32 devices in a mesh: chan: 16 (over z, y, core), tm: 2 (over x).
Axes of the slice: x: 2, y: 2, z: 4, core: 2. Of those that a mesh axis runs over, the one named last changes fastest.
Arguments:
- records: bfloat16 [6, 2048, 2048], P('tm', None, 'chan'), may hold values from -600 to 600
- band_taps: float32 [64], replicated, may hold values from -0.75 to 0.75
- white_taps: float32 [16, 2048], P(None, 'chan'), may hold values from -1.5 to 1.5
- live_mask: int32 [2048], P('chan'), may hold values 0 or 1
- partners: int32 [6, 16], P(None, 'chan'), may hold values from 0 to 15, as said below
Outputs:
- correlations: float32 [6, 32, 2048, 128], P(None, 'tm', 'chan')
The draws below stay inside these ranges and needn't reach their ends.
Inputs may be any that keep to these rules, and one draw needn't show every extreme that they name: In each round blocks are matched in pairs: partners[r, b] differs from b, partners[r, partners[r, b]] = b, and partners[r, b] - b equals d or -d modulo 16, with the same d in the finite set (1, 2, 4) for all blocks of the round. Over all rounds every block b is matched with b + 1, b - 1, b + 2, b - 2, b + 4 and b - 4 modulo 16, each once.
All inputs are finite; a program needn't handle non-finite values. No bound on the sum of `live_mask` on one device may be relied on, other than what follows from the above.
Results may differ from the reference program's by a relative error of at most 0.0058.
Values may be sent and summed in bfloat16 or wider, within the bound.
A program may use at most 64 MiB of HBM per device.

```python
import math
import jax
import jax.numpy as jnp
from jax import lax

CB = 128
SAMP = 2048
NB = 128
SEG = 6
BT = 64
WT = 16
ROUNDS = 6
LAGS = 32
BLOCKS = 16
CHANNELS = 2048


def draw_records(key, part):
    sub_keys = jax.random.split(key, 3)
    chan_scale = jnp.exp(jax.random.uniform(sub_keys[0], (1, 1, CHANNELS)) * math.log(10.0))
    seg_scale = jnp.exp(jax.random.uniform(sub_keys[1], (SEG, 1, CHANNELS)) * math.log(10.0))
    base_noise = jnp.clip(jax.random.normal(sub_keys[2], (SEG, SAMP, CHANNELS)), -6.0, 6.0)
    return (base_noise * chan_scale * seg_scale).astype(jnp.bfloat16)


def draw_partners(key, part):
    order = jax.random.permutation(jax.random.fold_in(key, 12), ROUNDS).astype(jnp.int32)
    distances = jnp.array([1, 1, 2, 2, 4, 4], dtype=jnp.int32)[order]
    phases = jnp.array([0, 1, 0, 1, 0, 1], dtype=jnp.int32)[order]
    block_ids = jnp.arange(BLOCKS, dtype=jnp.int32)[None, :]
    upward = jnp.mod(block_ids // distances[:, None], 2) == phases[:, None]
    mates = jnp.where(upward, block_ids + distances[:, None], block_ids - distances[:, None])
    return jnp.mod(mates, BLOCKS).astype(jnp.int32)


def plant(values, rng, smallest, top_value):
    extent = values.shape
    spot = [jax.random.randint(jax.random.fold_in(rng, axis), (), 0, extent[axis]) for axis in range(len(extent))]
    values = values.at[tuple(spot)].set(smallest)
    longest = extent.index(max(extent))
    spot[longest] = (spot[longest] + 1) % extent[longest]
    return values.at[tuple(spot)].set(top_value)


def block_levels(own_key, shape, pieces, low, top_value):
    loudness, own = 1.0, jax.random.fold_in(own_key, 6)
    for axis_at, shards_of in pieces:
        heights = jnp.exp(jax.random.uniform(jax.random.fold_in(own, axis_at), (shards_of,), jnp.float32, low / len(pieces), top_value / len(pieces)))
        loudness = loudness * jnp.repeat(heights, shape[axis_at] // shards_of).reshape([-1 if axis == axis_at else 1 for axis in range(len(shape))])
    return loudness


def noise(rng, shape, deviation, reach, cuts=(), kind=jnp.bfloat16):
    values = deviation * jax.random.normal(rng, shape, jnp.float32)
    if cuts:
        values = values * block_levels(rng, shape, cuts, -0.22, 0.18)
    return jnp.clip(values, -reach, reach).astype(kind)


def setup_inputs(seed: int = 0) -> dict:
    key_list = jax.random.split(jax.random.key(seed), 6)
    return {
        "records": draw_records(jax.random.fold_in(key_list[5], 71), 0),
        "band_taps": noise(key_list[1], (BT,), BT ** -0.5, 0.75, (), jnp.float32),
        "white_taps": noise(key_list[2], (WT, CHANNELS), WT ** -0.5, 1.5, ((1, 16),), jnp.float32),
        "live_mask": plant((jax.random.randint(key_list[3], (CHANNELS,), 0, 8) < 7).astype(jnp.int32), jax.random.fold_in(key_list[3], 1), 0, 1),
        "partners": draw_partners(jax.random.fold_in(key_list[5], 71), 0),
    }


def bin_numbers(samples, bin_count):
    return samples // 64 + samples // (4 * bin_count) * jnp.arange(bin_count, dtype=jnp.int32)

def rotation(products, samples):
    angles = jnp.mod(products, samples).astype(jnp.float32) * (2.0 * math.pi / samples)
    return (jnp.cos(angles), jnp.sin(angles))

def dft_table(samples, bin_index):
    sample_index = jnp.arange(samples, dtype=jnp.int32)
    cos_part, sin_part = rotation(sample_index[:, None] * bin_index[None, :], samples)
    return jnp.concatenate([cos_part, -sin_part], axis=1).astype(jnp.bfloat16)

def responses(band_taps, white_taps, bin_index, samples):
    highest = lax.Precision.HIGHEST
    band_cos, band_sin = rotation(jnp.arange(band_taps.shape[0], dtype=jnp.int32)[:, None] * bin_index[None, :], samples)
    white_cos, white_sin = rotation(jnp.arange(white_taps.shape[0], dtype=jnp.int32)[:, None] * bin_index[None, :], samples)
    band_real = jnp.dot(band_taps, band_cos, precision=highest)
    band_imag = -jnp.dot(band_taps, band_sin, precision=highest)
    white_real = jnp.dot(white_taps.T, white_cos, precision=highest)
    white_imag = -jnp.dot(white_taps.T, white_sin, precision=highest)
    resp_real = white_real * band_real[None, :] - white_imag * band_imag[None, :]
    resp_imag = white_real * band_imag[None, :] + white_imag * band_real[None, :]
    return (resp_real, resp_imag)

def filtered(raw_spec, resp_real, resp_imag, live_values):
    bin_count = resp_real.shape[1]
    spec_real = raw_spec[..., :bin_count]
    spec_imag = raw_spec[..., bin_count:]
    real_resp = resp_real[:, None, :]
    imag_resp = resp_imag[:, None, :]
    out_real = (real_resp * spec_real - imag_resp * spec_imag) * live_values[:, None, None]
    out_imag = (real_resp * spec_imag + imag_resp * spec_real) * live_values[:, None, None]
    return jnp.concatenate([out_real, out_imag], axis=2).astype(jnp.bfloat16)

def inverse_norms(flat_rows):
    values = flat_rows.astype(jnp.float32)
    mean_square = lax.optimization_barrier(jnp.sum(values * values, axis=-1)) / (SEG * NB)
    return lax.rsqrt(mean_square + 1e-06)

def turned_rows(own_block, lag_values, bin_index, samples):
    lag_cos, lag_sin = rotation(lag_values[:, None] * bin_index[None, :], samples)
    values = own_block.astype(jnp.float32).reshape(own_block.shape[0], SEG, 2, NB)
    part_real = values[:, :, 0, :][None]
    part_imag = values[:, :, 1, :][None]
    cos_factor = lag_cos[:, None, None, :]
    sin_factor = lag_sin[:, None, None, :]
    new_real = part_real * cos_factor - part_imag * sin_factor
    new_imag = part_real * sin_factor + part_imag * cos_factor
    stacked = jnp.stack([new_real, new_imag], axis=3)
    return stacked.astype(jnp.bfloat16).reshape(lag_values.shape[0] * own_block.shape[0], -1)

def tile_sums(turned, chosen, own_scale, part_scale, lag_count):
    rounds, row_count, inner_size = chosen.shape
    flat_rows = chosen.reshape(rounds * row_count, inner_size)
    tile_totals = lax.dot_general(turned, flat_rows, (((1,), (1,)), ((), ())), preferred_element_type=jnp.float32)
    tile_totals = tile_totals.reshape(lag_count, row_count, rounds, row_count)
    scaled = tile_totals * own_scale[None, :, None, None] * part_scale[None, None, :, :] * (1.0 / math.sqrt(SEG * NB))
    return jnp.transpose(scaled, (2, 0, 1, 3))

def reference(records, band_taps, white_taps, live_mask, partners):
    samples = records.shape[1]
    bin_index = bin_numbers(samples, NB)
    transform = dft_table(samples, bin_index)
    resp_real, resp_imag = responses(band_taps, white_taps, bin_index, samples)
    live_values = live_mask.astype(jnp.float32)

    def one_segment(segment_data):
        raw_spec = jnp.dot(segment_data.T, transform, preferred_element_type=jnp.float32)
        return filtered(raw_spec[:, None, :], resp_real, resp_imag, live_values)[:, 0, :]
    per_seg = lax.map(one_segment, records)
    spectra = jnp.transpose(per_seg, (1, 0, 2)).reshape(CHANNELS, SEG * 2 * NB)
    scales = inverse_norms(spectra)
    blocks = spectra.reshape(BLOCKS, CB, SEG * 2 * NB)
    block_scales = scales.reshape(BLOCKS, CB)
    lag_values = 3 * (jnp.arange(LAGS, dtype=jnp.int32) - LAGS // 2)

    def one_block(block_index):
        own_block = blocks[block_index]
        mate_index = partners[:, block_index]
        chosen = blocks[mate_index]
        turned = turned_rows(own_block, lag_values, bin_index, samples)
        return tile_sums(turned, chosen, block_scales[block_index], block_scales[mate_index], LAGS)
    all_tiles = lax.map(one_block, jnp.arange(BLOCKS, dtype=jnp.int32))
    return jnp.transpose(all_tiles, (1, 2, 0, 3, 4)).reshape(ROUNDS, LAGS, CHANNELS, CB)
```

```python
import functools
import math

import jax
import jax.numpy as jnp
import numpy as np
from jax import lax
from jax.experimental import pallas as pl
from jax.experimental.pallas import tpu as pltpu
from jax.sharding import PartitionSpec as P

NB = 128
SEG = 6
LAGS = 32
ROUNDS = 6
GROUP = 4
MESH = pl.DeviceIdType.MESH
VMEM = pltpu.VMEM
SMEM = pltpu.SMEM
OFFSETS = (-4, -2, -1, 1, 2, 4)


def bin_numbers(samples):
    return samples // 64 + samples // (4 * NB) * np.arange(NB, dtype=np.int64)


def rotation(products, samples):
    angles = np.mod(products, samples) * (2.0 * math.pi / samples)
    return np.cos(angles), np.sin(angles)


def gather_kernel(
    count, segs,
    rec, table, band_cos, band_sin, white_cos, white_sin, band, white, live,
    win, own_t,
    own, send, recv_x, recv_w,
):
    me = lax.axis_index("chan")
    tm = lax.axis_index("tm")
    core = lax.rem(me, 2)
    side = lax.rem(me // 2, 2)
    up = lax.rem(me + 4, count)
    down = lax.rem(me + count - 4, count)
    sib = me + 1 - 2 * core
    across = me + 2 - 4 * side
    other = 1 - tm

    barrier = pltpu.get_barrier_semaphore()
    for peer in ((me, other), (up, tm), (down, tm), (across, tm), (sib, tm)):
        pl.semaphore_signal(barrier, inc=1, device_id=peer, device_id_type=MESH)

    def seg_at(i):
        return tm * segs + i if i < segs else other * segs + (i - segs)

    sends = []

    def start(src, dst, sem, peer):
        copy = pltpu.make_async_remote_copy(
            src_ref=src, dst_ref=dst, send_sem=send.at[len(sends)], recv_sem=sem,
            device_id=peer, device_id_type=MESH,
        )
        copy.start()
        sends.append(copy)

    def arrived(dst, sem):
        pltpu.make_async_remote_copy(
            src_ref=dst, dst_ref=dst, send_sem=send.at[0], recv_sem=sem,
            device_id=(me, other), device_id_type=MESH,
        ).wait_recv()

    def wait_win(slot, seg):
        arrived(win.at[slot, seg], recv_w.at[slot, seg])

    def spread(seg):
        for slot, peer in ((0, up), (5, down), (1 + 3 * side, across), (2 + core, sib)):
            start(own.at[seg], win.at[slot, seg], recv_w.at[slot, seg], (peer, tm))

    relay_src, relay_dst = 5 - 5 * side, 4 - 3 * side
    pass_src, pass_dst = 4 - 3 * core, 3 - core

    def relay(seg):
        wait_win(relay_src, seg)
        start(win.at[relay_src, seg], win.at[relay_dst, seg], recv_w.at[relay_dst, seg], (across, tm))

    def hand_on(seg):
        wait_win(pass_src, seg)
        start(win.at[pass_src, seg], win.at[pass_dst, seg], recv_w.at[pass_dst, seg], (sib, tm))

    taps = band[...]
    band_re = jnp.sum(band_cos[...] * taps, axis=1, keepdims=True)
    band_im = -jnp.sum(band_sin[...] * taps, axis=1, keepdims=True)
    highest = lax.Precision.HIGHEST
    white_re = jnp.dot(white_cos[...], white[...], precision=highest, preferred_element_type=jnp.float32)
    white_im = -jnp.dot(white_sin[...], white[...], precision=highest, preferred_element_type=jnp.float32)
    resp_re = white_re * band_re - white_im * band_im
    resp_im = white_re * band_im + white_im * band_re
    alive = live[...].astype(jnp.float32)

    period = table.shape[1]
    for i in range(segs):
        raw = jnp.zeros((2 * NB, rec.shape[2]), jnp.float32)
        for first in range(0, rec.shape[1], period):
            raw = raw + jnp.dot(
                table[...], rec[i, first:first + period, :], preferred_element_type=jnp.float32
            )
        raw_re, raw_im = raw[:NB], raw[NB:]
        seg = seg_at(i)
        own[seg, :NB, :] = ((resp_re * raw_re - resp_im * raw_im) * alive).astype(jnp.bfloat16)
        own[seg, NB:, :] = ((resp_re * raw_im + resp_im * raw_re) * alive).astype(jnp.bfloat16)
        if i == 0:
            pl.semaphore_wait(barrier, 5)
        start(own.at[seg], own.at[seg], recv_x.at[i], (me, other))
        spread(seg)

    for i in range(segs):
        seg = seg_at(segs + i)
        arrived(own.at[seg], recv_x.at[i])
        spread(seg)
        relay(seg_at(i))
        if i:
            hand_on(seg_at(i - 1))
    for i in range(segs, 2 * segs):
        relay(seg_at(i))
        hand_on(seg_at(i - 1))
        if i == segs:
            for s in range(2 * segs):
                for part in range(2):
                    rows = own[s, part * NB:(part + 1) * NB, :].astype(jnp.float32)
                    at = (2 * s + part) * NB
                    own_t[:, at:at + NB] = rows.T.astype(jnp.bfloat16)
    hand_on(seg_at(2 * segs - 1))

    for i in range(2 * segs):
        for slot in (5 * side, 1 + 3 * core, 2, 3):
            wait_win(slot, seg_at(i))
    for copy in sends:
        copy.wait_send()


def correlate_kernel(count, place, partners, lag_table, own_t, win, out, wide, turned, scale_own, scale_win):
    step = pl.program_id(0)
    me = place[0]
    lag_first = place[1] * (LAGS // 2) + step * GROUP
    channels = own_t.shape[0]
    inner = own_t.shape[1]

    @pl.when(step == 0)
    def _():
        values = own_t[...].astype(jnp.float32)
        wide[...] = values
        mean_square = jnp.sum(values * values, axis=1, keepdims=True) / (SEG * NB)
        scale_own[...] = lax.rsqrt(mean_square + 1e-06) * (1.0 / math.sqrt(SEG * NB))
        for slot in range(len(OFFSETS)):
            rows = win[slot].astype(jnp.float32)
            total = jnp.sum(jnp.sum(rows * rows, axis=0), axis=0, keepdims=True) / (SEG * NB)
            scale_win[slot] = lax.rsqrt(total + 1e-06)

    for l in range(GROUP):
        pair = lag_table[lag_first + l]
        cos, sin = pair[0:1], pair[1:2]
        rows = slice(l * channels, (l + 1) * channels)
        for s in range(SEG):
            at = 2 * s * NB
            re, im = wide[:, at:at + NB], wide[:, at + NB:at + 2 * NB]
            turned[rows, at:at + NB] = (re * cos - im * sin).astype(jnp.bfloat16)
            turned[rows, at + NB:at + 2 * NB] = (re * sin + im * cos).astype(jnp.bfloat16)

    def slot_of(r):
        delta = lax.rem(partners[r, 0] - me + count + count // 2, count) - count // 2
        slot = jnp.int32(0)
        for position, offset in enumerate(OFFSETS):
            slot = slot + jnp.where(delta == offset, position, 0)
        return slot

    own_scale = scale_own[...]
    for r in range(0, ROUNDS, 2):
        slots = (slot_of(r), slot_of(r + 1))
        chosen = jnp.concatenate([win[s].reshape(inner, channels) for s in slots], axis=1)
        sums = jnp.dot(turned[...], chosen, preferred_element_type=jnp.float32)
        for k in range(2):
            part = sums[:, k * channels:(k + 1) * channels].reshape(GROUP, channels, channels)
            out[r + k] = part * own_scale[None] * scale_win[slots[k]][None]


def local(records, band_taps, white_taps, live_mask, partners):
    segs, samples, channels = records.shape
    count = lax.axis_size("chan")
    inner = SEG * 2 * NB
    lag_count = LAGS // lax.axis_size("tm")
    bins = bin_numbers(samples)
    period = samples // math.gcd(samples, math.gcd(int(bins[0]), int(bins[1] - bins[0])))
    cos, sin = rotation(bins[:, None] * np.arange(period)[None, :], samples)
    table = np.concatenate([cos, -sin], axis=0).astype(np.float32).astype(jnp.bfloat16)
    band_cos, band_sin = rotation(bins[:, None] * np.arange(band_taps.shape[0])[None, :], samples)
    white_cos, white_sin = rotation(bins[:, None] * np.arange(white_taps.shape[0])[None, :], samples)
    f32 = lambda a: jnp.asarray(a.astype(np.float32))

    vmem = pl.BlockSpec(memory_space=VMEM)
    win, own_t = pl.pallas_call(
        functools.partial(gather_kernel, count, segs),
        out_shape=(
            jax.ShapeDtypeStruct((6, SEG, 2 * NB, channels), jnp.bfloat16),
            jax.ShapeDtypeStruct((channels, inner), jnp.bfloat16),
        ),
        in_specs=[vmem] * 9,
        out_specs=(pl.BlockSpec(memory_space=pl.ANY), vmem),
        scratch_shapes=[
            VMEM((SEG, 2 * NB, channels), jnp.bfloat16),
            pltpu.SemaphoreType.DMA((segs + 6 * SEG,)),
            pltpu.SemaphoreType.DMA((segs,)),
            pltpu.SemaphoreType.DMA((6, SEG)),
        ],
        compiler_params=pltpu.CompilerParams(
            collective_id=0, has_side_effects=True, vmem_limit_bytes=32 * 1024 * 1024
        ),
        name="spectra_gather",
    )(
        records, jnp.asarray(table), f32(band_cos), f32(band_sin), f32(white_cos), f32(white_sin),
        band_taps.reshape(1, -1), white_taps, live_mask.reshape(1, -1),
    )

    lags = 3 * (np.arange(LAGS) - LAGS // 2)
    lag_table = np.stack(rotation(lags[:, None] * bins[None, :], samples), axis=1)
    place = jnp.stack([lax.axis_index("chan"), lax.axis_index("tm")]).astype(jnp.int32)
    whole = lambda *shape: pl.BlockSpec(shape, lambda i: (0,) * len(shape))
    smem = pl.BlockSpec(memory_space=SMEM)
    return pl.pallas_call(
        functools.partial(correlate_kernel, count),
        grid=(lag_count // GROUP,),
        out_shape=jax.ShapeDtypeStruct((ROUNDS, lag_count, channels, channels), jnp.float32),
        in_specs=[
            smem, smem, whole(LAGS, 2, NB), whole(channels, inner),
            whole(6, SEG, 2 * NB, channels),
        ],
        out_specs=pl.BlockSpec((ROUNDS, GROUP, channels, channels), lambda i: (0, i, 0, 0)),
        scratch_shapes=[
            VMEM((channels, inner), jnp.float32),
            VMEM((GROUP * channels, inner), jnp.bfloat16),
            VMEM((channels, 1), jnp.float32),
            VMEM((6, 1, channels), jnp.float32),
        ],
        compiler_params=pltpu.CompilerParams(vmem_limit_bytes=48 * 1024 * 1024),
        name="correlate",
    )(place, partners, f32(lag_table), own_t, win)


def solution(mesh):
    return jax.shard_map(
        local,
        mesh=mesh,
        in_specs=(P("tm", None, "chan"), P(), P(None, "chan"), P("chan"), P(None, "chan")),
        out_specs=P(None, "tm", "chan", None),
        check_vma=False,
    )
```

```python
import functools
import math

import jax
import jax.numpy as jnp
import numpy as np
from jax import lax
from jax.experimental import pallas as pl
from jax.experimental.pallas import tpu as pltpu
from jax.sharding import PartitionSpec as P

NB = 128
SEG = 6
LAGS = 32
ROUNDS = 6
GROUP = 4
MESH = pl.DeviceIdType.MESH
VMEM = pltpu.VMEM
SMEM = pltpu.SMEM
ROLES = 6
WHOLE_VMEM = 63_480_000


def bin_numbers(samples):
    return samples // 64 + samples // (4 * NB) * np.arange(NB, dtype=np.int64)


def rotation(products, samples):
    angles = np.mod(products, samples) * (2.0 * math.pi / samples)
    return np.cos(angles), np.sin(angles)


def gather_kernel(
    count, segs,
    rec_in, table_in, band_table_in, white_table_in, lag_table_in, band_in, white_in, live_in,
    products,
    own, win, turned, staged, rec, table, band_table, white_table, lag_table, band, white, live,
    fetch, send, recv_x, recv_w, put,
):
    me = lax.axis_index("chan")
    tm = lax.axis_index("tm")
    core = lax.rem(me, 2)
    side = lax.rem(me // 2, 2)
    up = lax.rem(me + 4, count)
    down = lax.rem(me + count - 4, count)
    sib = me + 1 - 2 * core
    across = me + 2 - 4 * side
    other = 1 - tm
    lag_count, channels = lag_table.shape[0], own.shape[2]

    barrier = pltpu.get_barrier_semaphore()
    for peer in ((me, other), (up, tm), (down, tm), (across, tm), (sib, tm)):
        pl.semaphore_signal(barrier, inc=1, device_id=peer, device_id_type=MESH)

    pairs = [(band_in, band), (white_in, white), (live_in, live), (band_table_in, band_table),
             (white_table_in, white_table), (table_in, table)]
    pairs += [(rec_in.at[i], rec.at[i]) for i in range(segs)]
    pairs += [(lag_table_in.at[pl.ds(tm * lag_count, lag_count)], lag_table)]
    fetches = [pltpu.make_async_copy(src, dst, fetch.at[i]) for i, (src, dst) in enumerate(pairs)]
    for copy in fetches:
        copy.start()

    def seg_at(i):
        return tm * segs + i if i < segs else other * segs + (i - segs)

    sends = []

    def start(src, dst, sem, peer):
        copy = pltpu.make_async_remote_copy(
            src_ref=src, dst_ref=dst, send_sem=send.at[len(sends)], recv_sem=sem,
            device_id=peer, device_id_type=MESH,
        )
        copy.start()
        sends.append(copy)

    def arrived(dst, sem):
        pltpu.make_async_remote_copy(
            src_ref=dst, dst_ref=dst, send_sem=send.at[0], recv_sem=sem,
            device_id=(me, other), device_id_type=MESH,
        ).wait_recv()

    def wait_win(role, seg):
        arrived(win.at[role, seg], recv_w.at[role, seg])

    def spread(seg):
        for role, peer in ((2, up), (3, down), (1, across), (0, sib)):
            start(own.at[seg], win.at[role, seg], recv_w.at[role, seg], (peer, tm))

    mixed = lax.rem(core + side, 2)
    relay_src = 3 - side
    passing = segs + 5 * SEG

    def relay(i):
        seg = seg_at(i)
        wait_win(relay_src, seg)
        start(win.at[relay_src, seg], win.at[4, seg], recv_w.at[4, seg], (across, tm))

    def hand_on(role, i):
        seg = seg_at(i)
        wait_win(role, seg)

        @pl.when(mixed == role // 4)
        def _():
            pltpu.make_async_remote_copy(
                src_ref=win.at[role, seg], dst_ref=win.at[5, seg], send_sem=send.at[passing + i],
                recv_sem=recv_w.at[5, seg], device_id=(sib, tm), device_id_type=MESH,
            ).start()

    for copy in fetches[:5]:
        copy.wait()
    taps, band_count = band[...], band.shape[1]
    band_re = jnp.sum(band_table[:, :band_count] * taps, axis=1, keepdims=True)
    band_im = -jnp.sum(band_table[:, band_count:] * taps, axis=1, keepdims=True)
    white_resp = jnp.dot(
        white_table[...], white[...], precision=lax.Precision.HIGHEST, preferred_element_type=jnp.float32
    )
    white_re, white_im = white_resp[:NB], -white_resp[NB:]
    alive = live[...].astype(jnp.float32)
    resp_re = white_re * band_re - white_im * band_im
    resp_im = white_re * band_im + white_im * band_re

    period = table.shape[1]
    fetches[5].wait()
    for i in range(segs):
        fetches[6 + i].wait()
        raw = jnp.zeros((2 * NB, channels), jnp.float32)
        for first in range(0, rec.shape[1], period):
            raw = raw + jnp.dot(
                table[...], rec[i, first:first + period, :], preferred_element_type=jnp.float32
            )
        raw_re, raw_im = raw[:NB], raw[NB:]
        seg = seg_at(i)
        own[seg, :NB, :] = ((resp_re * raw_re - resp_im * raw_im) * alive).astype(jnp.bfloat16)
        own[seg, NB:, :] = ((resp_re * raw_im + resp_im * raw_re) * alive).astype(jnp.bfloat16)
        if i == 0:
            pl.semaphore_wait(barrier, 5)
        start(own.at[seg], own.at[seg], recv_x.at[i], (me, other))
        spread(seg)
    fetches[-1].wait()

    squares_own = jnp.zeros((channels, NB), jnp.float32)
    puts = []

    def turn(seg, total):
        re = own[seg, :NB, :].astype(jnp.float32).T
        im = own[seg, NB:, :].astype(jnp.float32).T
        at = pl.multiple_of(seg * 2 * NB, 2 * NB)

        def one_lag(l, carry):
            pair = lag_table[l]
            cos, sin = pair[0:1], pair[1:2]
            rows = pl.ds(pl.multiple_of(l * channels, channels), channels)
            turned[rows, pl.ds(at, NB)] = (re * cos - im * sin).astype(jnp.bfloat16)
            turned[rows, pl.ds(at + NB, NB)] = (re * sin + im * cos).astype(jnp.bfloat16)
            return carry

        lax.fori_loop(0, lag_count, one_lag, 0)
        return total + (re * re + im * im)

    def scales(roles, waited=None):
        squares = [jnp.zeros((8, channels), jnp.float32) for _ in roles]
        for i in range(2 * segs):
            seg = seg_at(i)
            if waited is not None:
                wait_win(waited, seg)
            for k, role in enumerate(roles):
                rows = win[role, seg].astype(jnp.float32)
                squares[k] += jnp.sum((rows * rows).reshape(-1, 8, channels), axis=0)
        means = [jnp.sum(part, axis=0, keepdims=True) / (SEG * NB) for part in squares]
        return jnp.concatenate([lax.rsqrt(mean + 1e-06) for mean in means], axis=1)

    def multiply(roles, scale, first, last):
        factor = own_scale * scale

        def one_group(g, carry):
            lags = pl.ds(g * GROUP, GROUP)
            rows = pl.ds(pl.multiple_of(g * GROUP * channels, GROUP * channels), GROUP * channels)
            chosen = jnp.concatenate([win[role].reshape(-1, channels) for role in roles], axis=1)
            sums = jnp.dot(turned[rows, :], chosen, preferred_element_type=jnp.float32)
            sums = sums.reshape(GROUP, channels, 2 * channels) * factor[None]
            for k, role in enumerate(roles):
                staged[role, lags] = sums[:, :, k * channels:(k + 1) * channels]
            return carry

        lax.fori_loop(first, last, one_group, 0)
        lags = pl.ds(first * GROUP, (last - first) * GROUP)
        for role in roles:
            copy = pltpu.make_async_copy(staged.at[role, lags], products.at[role, lags], put.at[len(puts)])
            copy.start()
            puts.append(copy)

    groups = lag_count // GROUP
    half = groups // 2
    for i in range(segs):
        seg = seg_at(segs + i)
        arrived(own.at[seg], recv_x.at[i])
        spread(seg)
        relay(i)
        hand_on(1, i)
        if i:
            hand_on(4, i - 1)
        squares_own = turn(seg_at(i), squares_own)
    relay(segs)
    hand_on(4, segs - 1)
    hand_on(1, segs)
    squares_own = turn(seg_at(segs), squares_own)
    squares_own = turn(seg_at(segs + 1), squares_own)
    relay(segs + 1)
    hand_on(4, segs)
    hand_on(1, segs + 1)
    hand_on(1, segs + 2)
    squares_own = turn(seg_at(segs + 2), squares_own)
    own_mean = jnp.sum(squares_own, axis=1, keepdims=True) / (SEG * NB)
    own_scale = lax.rsqrt(own_mean + 1e-06) * (1.0 / math.sqrt(SEG * NB))
    scale = scales((0, 1), 0)
    multiply((0, 1), scale, 0, groups)
    relay(segs + 2)
    hand_on(4, segs + 1)
    scale = scales((2, 3), 2 + side)
    multiply((2, 3), scale, 0, half)
    hand_on(4, segs + 2)
    multiply((2, 3), scale, half, groups)
    scale = scales((4, 5), 5)
    multiply((4, 5), scale, 0, half)
    multiply((4, 5), scale, half, groups)
    for copy in sends:
        copy.wait_send()
    for i in range(2 * segs):
        block = win.at[5, seg_at(i)]
        pltpu.make_async_remote_copy(
            src_ref=block, dst_ref=block, send_sem=send.at[passing + i], recv_sem=recv_w.at[5, seg_at(i)],
            device_id=(sib, tm), device_id_type=MESH,
        ).wait_send()
    for copy in puts:
        copy.wait()


def order_kernel(count, place, partners, products, out, sems):
    me = place[0]
    core = lax.rem(me, 2)
    side = lax.rem(me // 2, 2)
    offsets = (1 - 2 * core, 2 - 4 * side, -4, 4, 4 * side - 2, 2 * core - 1)
    copies = []
    for r in range(ROUNDS):
        delta = lax.rem(partners[r] - me + count + count // 2, count) - count // 2
        role = jnp.int32(0)
        for position, offset in enumerate(offsets):
            role = role + jnp.where(delta == offset, position, 0)
        for part in range(2):
            lags = pl.ds(part * (out.shape[1] // 2), out.shape[1] // 2)
            copies.append(pltpu.make_async_copy(products.at[role, lags], out.at[r, lags], sems.at[2 * r + part]))
            copies[-1].start()
    for copy in copies:
        copy.wait()


def local(records, band_taps, white_taps, live_mask, partners):
    segs, samples, channels = records.shape
    count = lax.axis_size("chan")
    inner = SEG * 2 * NB
    lag_count = LAGS // lax.axis_size("tm")
    bins = bin_numbers(samples)
    period = samples // math.gcd(samples, math.gcd(int(bins[0]), int(bins[1] - bins[0])))
    cos, sin = rotation(bins[:, None] * np.arange(period)[None, :], samples)
    table = np.concatenate([cos, -sin], axis=0).astype(np.float32).astype(jnp.bfloat16)
    band_table = np.concatenate(rotation(bins[:, None] * np.arange(band_taps.shape[0])[None, :], samples), axis=1)
    white_table = np.concatenate(rotation(bins[:, None] * np.arange(white_taps.shape[0])[None, :], samples), axis=0)
    lags = 3 * (np.arange(LAGS) - LAGS // 2)
    lag_table = np.stack(rotation(lags[:, None] * bins[None, :], samples), axis=1)
    f32 = lambda a: jnp.asarray(a.astype(np.float32))
    operands = (
        records, jnp.asarray(table), f32(band_table), f32(white_table), f32(lag_table),
        band_taps.reshape(1, -1), white_taps, live_mask.reshape(1, -1),
    )

    hbm = pl.BlockSpec(memory_space=pltpu.HBM)
    smem = pl.BlockSpec(memory_space=SMEM)
    shape = jax.ShapeDtypeStruct((ROLES, lag_count, channels, channels), jnp.float32)
    products = pl.pallas_call(
        functools.partial(gather_kernel, count, segs),
        out_shape=shape,
        in_specs=[hbm] * len(operands),
        out_specs=hbm,
        scratch_shapes=[
            VMEM((SEG, 2 * NB, channels), jnp.bfloat16),
            VMEM((ROLES, SEG, 2 * NB, channels), jnp.bfloat16),
            VMEM((lag_count * channels, inner), jnp.bfloat16),
            VMEM(shape.shape, jnp.float32),
            VMEM(records.shape, jnp.bfloat16),
            VMEM(table.shape, jnp.bfloat16),
            VMEM(band_table.shape, jnp.float32),
            VMEM(white_table.shape, jnp.float32),
            VMEM((lag_count, 2, NB), jnp.float32),
            VMEM((1, band_taps.shape[0]), jnp.float32),
            VMEM(white_taps.shape, jnp.float32),
            VMEM((1, channels), jnp.int32),
            pltpu.SemaphoreType.DMA((7 + segs,)),
            pltpu.SemaphoreType.DMA((segs + 6 * SEG,)),
            pltpu.SemaphoreType.DMA((segs,)),
            pltpu.SemaphoreType.DMA((ROLES, SEG)),
            pltpu.SemaphoreType.DMA((10,)),
        ],
        compiler_params=pltpu.CompilerParams(
            collective_id=0, has_side_effects=True, vmem_limit_bytes=WHOLE_VMEM
        ),
        name="spectra_gather",
    )(*operands)

    place = lax.axis_index("chan").astype(jnp.int32).reshape(1)
    return pl.pallas_call(
        functools.partial(order_kernel, count),
        out_shape=shape,
        in_specs=[smem, smem, hbm],
        out_specs=hbm,
        scratch_shapes=[pltpu.SemaphoreType.DMA((2 * ROUNDS,))],
        compiler_params=pltpu.CompilerParams(vmem_limit_bytes=WHOLE_VMEM),
        name="round_order",
    )(place, partners.reshape(-1), products)


def solution(mesh):
    return jax.shard_map(
        local,
        mesh=mesh,
        in_specs=(P("tm", None, "chan"), P(), P(None, "chan"), P("chan"), P(None, "chan")),
        out_specs=P(None, "tm", "chan", None),
        check_vma=False,
    )
```

```python
import functools
import math

import jax
import jax.numpy as jnp
import numpy as np
from jax import lax
from jax.experimental import pallas as pl
from jax.experimental.pallas import tpu as pltpu
from jax.sharding import PartitionSpec as P

NB = 128
SEG = 6
LAGS = 32
ROUNDS = 6
GROUP = 8
MESH = pl.DeviceIdType.MESH
VMEM = pltpu.VMEM
SMEM = pltpu.SMEM
ROLES = 6
WHOLE_VMEM = 63_480_000


def bin_numbers(samples):
    return samples // 64 + samples // (4 * NB) * np.arange(NB, dtype=np.int64)


def rotation(products, samples):
    angles = np.mod(products, samples) * (2.0 * math.pi / samples)
    return np.cos(angles), np.sin(angles)


def gather_kernel(
    count, segs,
    rec_in, table_in, band_table_in, white_table_in, lag_table_in, band_in, white_in, live_in,
    products,
    own, win, turned, staged, rec, table, band_table, white_table, lag_table, band, white, live,
    fetch, send, recv_x, recv_w, put,
):
    me = lax.axis_index("chan")
    tm = lax.axis_index("tm")
    core = lax.rem(me, 2)
    side = lax.rem(me // 2, 2)
    up = lax.rem(me + 4, count)
    down = lax.rem(me + count - 4, count)
    sib = me + 1 - 2 * core
    across = me + 2 - 4 * side
    other = 1 - tm
    lag_count, channels = lag_table.shape[0], own.shape[2]

    barrier = pltpu.get_barrier_semaphore()
    for peer in ((me, other), (up, tm), (down, tm), (across, tm), (sib, tm)):
        pl.semaphore_signal(barrier, inc=1, device_id=peer, device_id_type=MESH)

    pairs = [(band_in, band), (white_in, white), (live_in, live), (band_table_in, band_table),
             (white_table_in, white_table), (table_in, table)]
    pairs += [(rec_in.at[i], rec.at[i]) for i in range(segs)]
    pairs += [(lag_table_in.at[pl.ds(tm * lag_count, lag_count)], lag_table)]
    fetches = [pltpu.make_async_copy(src, dst, fetch.at[i]) for i, (src, dst) in enumerate(pairs)]
    for copy in fetches:
        copy.start()

    def seg_at(i):
        return tm * segs + i if i < segs else other * segs + (i - segs)

    sends = []

    def start(src, dst, sem, peer, only=None):
        copy = pltpu.make_async_remote_copy(
            src_ref=src, dst_ref=dst, send_sem=send.at[len(sends)], recv_sem=sem,
            device_id=peer, device_id_type=MESH,
        )
        sends.append((copy, only))
        if only is None:
            copy.start()
        else:
            pl.when(only)(copy.start)

    def arrived(dst, sem):
        pltpu.make_async_remote_copy(
            src_ref=dst, dst_ref=dst, send_sem=send.at[0], recv_sem=sem,
            device_id=(me, other), device_id_type=MESH,
        ).wait_recv()

    def wait_win(role, seg):
        arrived(win.at[role, seg], recv_w.at[role, seg])

    first_row, last_row = me < 4, me >= count - 4
    mixed = lax.rem(core + side, 2)
    relay_src = 3 - side
    beyond = jnp.where(first_row, 2, 3)

    def send_win(src, role, seg, peer, only=None):
        start(src, win.at[role, seg], recv_w.at[role, seg], peer, only)

    def spread(i):
        seg = seg_at(i)
        second = i >= segs
        send_win(own.at[seg], 2, seg, (up, tm), jnp.logical_not(last_row) if second else None)
        send_win(own.at[seg], 3, seg, (down, tm), jnp.logical_not(first_row) if second else None)
        if not second:
            send_win(own.at[seg], 1, seg, (across, tm))
        send_win(own.at[seg], 0, seg, (sib, tm))

    def relay(i):
        seg = seg_at(i)
        for role in (2, 3):
            wait_win(role, seg)
        send_win(win.at[relay_src, seg], 4, seg, (across, tm))
        if i < segs:
            send_win(win.at[beyond, seg], beyond, seg, (me, other), jnp.logical_or(first_row, last_row))

    def hand_on(role, i):
        seg = seg_at(i)
        wait_win(role, seg)
        if role == 1 and i < segs:
            send_win(win.at[1, seg], 1, seg, (me, other))
        send_win(win.at[role, seg], 5, seg, (sib, tm), mixed == role // 4)

    for copy in fetches[:5]:
        copy.wait()
    taps, band_count = band[...], band.shape[1]
    band_re = jnp.sum(band_table[:, :band_count] * taps, axis=1, keepdims=True)
    band_im = -jnp.sum(band_table[:, band_count:] * taps, axis=1, keepdims=True)
    white_resp = jnp.dot(
        white_table[...], white[...], precision=lax.Precision.HIGHEST, preferred_element_type=jnp.float32
    )
    white_re, white_im = white_resp[:NB], -white_resp[NB:]
    alive = live[...].astype(jnp.float32)
    resp_re = white_re * band_re - white_im * band_im
    resp_im = white_re * band_im + white_im * band_re

    period = table.shape[1]
    fetches[5].wait()
    for i in range(segs):
        fetches[6 + i].wait()
        raw = jnp.zeros((2 * NB, channels), jnp.float32)
        for first in range(0, rec.shape[1], period):
            raw = raw + jnp.dot(
                table[...], rec[i, first:first + period, :], preferred_element_type=jnp.float32
            )
        raw_re, raw_im = raw[:NB], raw[NB:]
        seg = seg_at(i)
        own[seg, :NB, :] = ((resp_re * raw_re - resp_im * raw_im) * alive).astype(jnp.bfloat16)
        own[seg, NB:, :] = ((resp_re * raw_im + resp_im * raw_re) * alive).astype(jnp.bfloat16)
        if i == 0:
            pl.semaphore_wait(barrier, 5)
        start(own.at[seg], own.at[seg], recv_x.at[i], (me, other))
        spread(i)
    fetches[-1].wait()

    squares_own = jnp.zeros((channels, NB), jnp.float32)
    puts = []

    def turn(seg, total):
        re = own[seg, :NB, :].astype(jnp.float32).T
        im = own[seg, NB:, :].astype(jnp.float32).T
        at = pl.multiple_of(seg * 2 * NB, 2 * NB)

        def one_lag(l, carry):
            pair = lag_table[l]
            cos, sin = pair[0:1], pair[1:2]
            rows = pl.ds(pl.multiple_of(l * channels, channels), channels)
            turned[rows, pl.ds(at, NB)] = (re * cos - im * sin).astype(jnp.bfloat16)
            turned[rows, pl.ds(at + NB, NB)] = (re * sin + im * cos).astype(jnp.bfloat16)
            return carry

        lax.fori_loop(0, lag_count, one_lag, 0)
        return total + (re * re + im * im)

    def add_squares(totals, roles, places, waited=None):
        totals = list(totals)
        for i in places:
            seg = seg_at(i)
            if waited is not None:
                wait_win(waited, seg)
            for k, role in enumerate(roles):
                rows = win[role, seg].astype(jnp.float32)
                totals[k] += jnp.sum((rows * rows).reshape(-1, 8, channels), axis=0)
        return totals

    def scales(totals):
        means = [jnp.sum(part, axis=0, keepdims=True) / (SEG * NB) for part in totals]
        return own_scale * jnp.concatenate([lax.rsqrt(mean + 1e-06) for mean in means], axis=1)

    def multiply(roles, which, factor=None, groups=None):
        span = pl.ds(which * segs, segs)
        columns = pl.ds(pl.multiple_of(which * segs * 2 * NB, 2 * NB), segs * 2 * NB)
        for g in groups or range(lag_count // GROUP):
            lags = pl.ds(g * GROUP, GROUP)
            rows = pl.ds(g * GROUP * channels, GROUP * channels)
            chosen = jnp.concatenate([win[role, span].reshape(-1, channels) for role in roles], axis=1)
            sums = jnp.dot(turned[rows, columns], chosen, preferred_element_type=jnp.float32)
            sums = sums.reshape(GROUP, channels, 2 * channels)
            for k, role in enumerate(roles):
                mine = slice(k * channels, (k + 1) * channels)
                if factor is None:
                    staged[role, lags] = sums[:, :, mine]
                else:
                    staged[role, lags] = (staged[role, lags] + sums[:, :, mine]) * factor[:, mine][None]
                    copy = pltpu.make_async_copy(
                        staged.at[role, lags], products.at[role, lags], put.at[len(puts)]
                    )
                    copy.start()
                    puts.append(copy)

    firsts, seconds = range(segs), range(segs, 2 * segs)
    nothing = [jnp.zeros((8, channels), jnp.float32)] * 2
    for i in firsts:
        arrived(own.at[seg_at(segs + i)], recv_x.at[i])
        spread(segs + i)
        relay(i)
        hand_on(1, i)
        if i:
            hand_on(4, i - 1)
        squares_own = turn(seg_at(i), squares_own)
    relay(segs)
    hand_on(4, segs - 1)
    hand_on(1, segs)
    multiply((2, 3), tm)
    squares_b = add_squares(nothing, (2, 3), firsts)
    squares_own = turn(seg_at(segs), squares_own)
    squares_own = turn(seg_at(segs + 1), squares_own)
    relay(segs + 1)
    hand_on(4, segs)
    hand_on(1, segs + 1)
    hand_on(1, segs + 2)
    squares_own = turn(seg_at(segs + 2), squares_own)
    own_mean = jnp.sum(squares_own, axis=1, keepdims=True) / (SEG * NB)
    own_scale = lax.rsqrt(own_mean + 1e-06) * (1.0 / math.sqrt(SEG * NB))
    squares_a = add_squares(nothing, (0, 1), range(2 * segs), 0)
    multiply((0, 1), tm)
    multiply((0, 1), other, scales(squares_a))
    relay(segs + 2)
    hand_on(4, segs + 1)
    squares_c = add_squares(nothing, (4, 5), firsts, 5)
    multiply((4, 5), tm)
    hand_on(4, segs + 2)
    squares_b = add_squares(squares_b, (2, 3), seconds)
    multiply((2, 3), other, scales(squares_b))
    squares_c = add_squares(squares_c, (4, 5), seconds, 5)
    multiply((4, 5), other, scales(squares_c))
    for copy, only in sends:
        if only is None:
            copy.wait_send()
        else:
            pl.when(only)(copy.wait_send)
    for copy in puts:
        copy.wait()


def order_kernel(count, place, partners, products, out, held, get, put):
    me = place[0]
    core = lax.rem(me, 2)
    side = lax.rem(me // 2, 2)
    offsets = (1 - 2 * core, 2 - 4 * side, -4, 4, 4 * side - 2, 2 * core - 1)
    part = out.shape[1] // 2
    gets, puts = [], []
    for r in range(ROUNDS):
        delta = lax.rem(partners[r] - me + count + count // 2, count) - count // 2
        role = jnp.int32(0)
        for position, offset in enumerate(offsets):
            role = role + jnp.where(delta == offset, position, 0)
        for h in range(2):
            k = 2 * r + h
            lags = pl.ds(h * part, part)
            gets.append(pltpu.make_async_copy(products.at[role, lags], held.at[r, lags], get.at[k]))
            puts.append(pltpu.make_async_copy(held.at[r, lags], out.at[r, lags], put.at[k]))
            gets[-1].start()
    for into, onward in zip(gets, puts):
        into.wait()
        onward.start()
    for onward in puts:
        onward.wait()


def local(records, band_taps, white_taps, live_mask, partners):
    segs, samples, channels = records.shape
    count = lax.axis_size("chan")
    inner = SEG * 2 * NB
    lag_count = LAGS // lax.axis_size("tm")
    bins = bin_numbers(samples)
    period = samples // math.gcd(samples, math.gcd(int(bins[0]), int(bins[1] - bins[0])))
    cos, sin = rotation(bins[:, None] * np.arange(period)[None, :], samples)
    table = np.concatenate([cos, -sin], axis=0).astype(np.float32).astype(jnp.bfloat16)
    band_table = np.concatenate(rotation(bins[:, None] * np.arange(band_taps.shape[0])[None, :], samples), axis=1)
    white_table = np.concatenate(rotation(bins[:, None] * np.arange(white_taps.shape[0])[None, :], samples), axis=0)
    lags = 3 * (np.arange(LAGS) - LAGS // 2)
    lag_table = np.stack(rotation(lags[:, None] * bins[None, :], samples), axis=1)
    f32 = lambda a: jnp.asarray(a.astype(np.float32))
    operands = (
        records, jnp.asarray(table), f32(band_table), f32(white_table), f32(lag_table),
        band_taps.reshape(1, -1), white_taps, live_mask.reshape(1, -1),
    )

    hbm = pl.BlockSpec(memory_space=pltpu.HBM)
    smem = pl.BlockSpec(memory_space=SMEM)
    shape = jax.ShapeDtypeStruct((ROLES, lag_count, channels, channels), jnp.float32)
    products = pl.pallas_call(
        functools.partial(gather_kernel, count, segs),
        out_shape=shape,
        in_specs=[hbm] * len(operands),
        out_specs=hbm,
        scratch_shapes=[
            VMEM((SEG, 2 * NB, channels), jnp.bfloat16),
            VMEM((ROLES, SEG, 2 * NB, channels), jnp.bfloat16),
            VMEM((lag_count * channels, inner), jnp.bfloat16),
            VMEM(shape.shape, jnp.float32),
            VMEM(records.shape, jnp.bfloat16),
            VMEM(table.shape, jnp.bfloat16),
            VMEM(band_table.shape, jnp.float32),
            VMEM(white_table.shape, jnp.float32),
            VMEM((lag_count, 2, NB), jnp.float32),
            VMEM((1, band_taps.shape[0]), jnp.float32),
            VMEM(white_taps.shape, jnp.float32),
            VMEM((1, channels), jnp.int32),
            pltpu.SemaphoreType.DMA((7 + segs,)),
            pltpu.SemaphoreType.DMA((segs + 8 * SEG,)),
            pltpu.SemaphoreType.DMA((segs,)),
            pltpu.SemaphoreType.DMA((ROLES, SEG)),
            pltpu.SemaphoreType.DMA((ROLES * lag_count // GROUP,)),
        ],
        compiler_params=pltpu.CompilerParams(
            collective_id=0, has_side_effects=True, vmem_limit_bytes=WHOLE_VMEM
        ),
        name="spectra_gather",
    )(*operands)

    place = lax.axis_index("chan").astype(jnp.int32).reshape(1)
    return pl.pallas_call(
        functools.partial(order_kernel, count),
        out_shape=shape,
        in_specs=[smem, smem, hbm],
        out_specs=hbm,
        scratch_shapes=[
            VMEM(shape.shape, jnp.float32),
            pltpu.SemaphoreType.DMA((2 * ROUNDS,)),
            pltpu.SemaphoreType.DMA((2 * ROUNDS,)),
        ],
        compiler_params=pltpu.CompilerParams(vmem_limit_bytes=WHOLE_VMEM),
        name="round_order",
    )(place, partners.reshape(-1), products)


def solution(mesh):
    return jax.shard_map(
        local,
        mesh=mesh,
        in_specs=(P("tm", None, "chan"), P(), P(None, "chan"), P("chan"), P(None, "chan")),
        out_specs=P(None, "tm", "chan", None),
        check_vma=False,
    )
```

```python
import functools
import math

import jax
import jax.numpy as jnp
import numpy as np
from jax import lax
from jax.experimental import pallas as pl
from jax.experimental.pallas import tpu as pltpu
from jax.sharding import PartitionSpec as P

NB = 128
SEG = 6
LAGS = 32
ROUNDS = 6
GROUP = 4
MESH = pl.DeviceIdType.MESH
VMEM = pltpu.VMEM
SMEM = pltpu.SMEM
ROLES = 6
WHOLE_VMEM = 63_480_000


def bin_numbers(samples):
    return samples // 64 + samples // (4 * NB) * np.arange(NB, dtype=np.int64)


def rotation(products, samples):
    angles = np.mod(products, samples) * (2.0 * math.pi / samples)
    return np.cos(angles), np.sin(angles)


def gather_kernel(
    count, segs,
    rec_in, table_in, band_table_in, white_table_in, lag_table_in, band_in, white_in, live_in,
    win, turned_out, scale_out,
    own, turned, own_scale, rec, table, band_table, white_table, lag_table, band, white, live,
    fetch, send, recv_x, recv_w, put,
):
    me = lax.axis_index("chan")
    tm = lax.axis_index("tm")
    core = lax.rem(me, 2)
    side = lax.rem(me // 2, 2)
    up = lax.rem(me + 4, count)
    down = lax.rem(me + count - 4, count)
    sib = me + 1 - 2 * core
    across = me + 2 - 4 * side
    other = 1 - tm
    lag_count, channels = lag_table.shape[0], own.shape[2]

    barrier = pltpu.get_barrier_semaphore()
    for peer in ((me, other), (up, tm), (down, tm), (across, tm), (sib, tm)):
        pl.semaphore_signal(barrier, inc=1, device_id=peer, device_id_type=MESH)

    pairs = [(band_in, band), (white_in, white), (live_in, live), (band_table_in, band_table),
             (white_table_in, white_table), (table_in, table)]
    pairs += [(rec_in.at[i], rec.at[i]) for i in range(segs)]
    pairs += [(lag_table_in.at[pl.ds(tm * lag_count, lag_count)], lag_table)]
    fetches = [pltpu.make_async_copy(src, dst, fetch.at[i]) for i, (src, dst) in enumerate(pairs)]
    for copy in fetches:
        copy.start()

    def seg_at(i):
        return tm * segs + i if i < segs else other * segs + (i - segs)

    sends = []

    def start(src, dst, sem, peer, only=None):
        copy = pltpu.make_async_remote_copy(
            src_ref=src, dst_ref=dst, send_sem=send.at[len(sends)], recv_sem=sem,
            device_id=peer, device_id_type=MESH,
        )
        sends.append((copy, only))
        if only is None:
            copy.start()
        else:
            pl.when(only)(copy.start)

    def arrived(dst, sem):
        pltpu.make_async_remote_copy(
            src_ref=dst, dst_ref=dst, send_sem=send.at[0], recv_sem=sem,
            device_id=(me, other), device_id_type=MESH,
        ).wait_recv()

    def wait_win(role, seg):
        arrived(win.at[role, seg], recv_w.at[role, seg])

    first_row, last_row = me < 4, me >= count - 4
    mixed = lax.rem(core + side, 2)
    relay_src = 3 - side
    beyond = jnp.where(first_row, 2, 3)

    def send_win(src, role, seg, peer, only=None):
        start(src, win.at[role, seg], recv_w.at[role, seg], peer, only)

    def spread(i):
        seg = seg_at(i)
        second = i >= segs
        send_win(own.at[seg], 2, seg, (up, tm), jnp.logical_not(last_row) if second else None)
        send_win(own.at[seg], 3, seg, (down, tm), jnp.logical_not(first_row) if second else None)
        if not second:
            send_win(own.at[seg], 1, seg, (across, tm))
        send_win(own.at[seg], 0, seg, (sib, tm))

    def relay(i):
        seg = seg_at(i)
        wait_win(relay_src, seg)
        send_win(win.at[relay_src, seg], 4, seg, (across, tm))
        wait_win(2 + side, seg)
        if i < segs:
            send_win(win.at[beyond, seg], beyond, seg, (me, other), jnp.logical_or(first_row, last_row))

    def hand_on(role, i):
        seg = seg_at(i)
        wait_win(role, seg)
        if role == 1 and i < segs:
            send_win(win.at[1, seg], 1, seg, (me, other))
        send_win(win.at[role, seg], 5, seg, (sib, tm), mixed == role // 4)

    for copy in fetches[:5]:
        copy.wait()
    taps, band_count = band[...], band.shape[1]
    band_re = jnp.sum(band_table[:, :band_count] * taps, axis=1, keepdims=True)
    band_im = -jnp.sum(band_table[:, band_count:] * taps, axis=1, keepdims=True)
    white_resp = jnp.dot(
        white_table[...], white[...], precision=lax.Precision.HIGHEST, preferred_element_type=jnp.float32
    )
    white_re, white_im = white_resp[:NB], -white_resp[NB:]
    alive = live[...].astype(jnp.float32)
    resp_re = white_re * band_re - white_im * band_im
    resp_im = white_re * band_im + white_im * band_re

    period = table.shape[1]
    fetches[5].wait()
    for i in range(segs):
        fetches[6 + i].wait()
        raw = jnp.zeros((2 * NB, channels), jnp.float32)
        for first in range(0, rec.shape[1], period):
            raw = raw + jnp.dot(
                table[...], rec[i, first:first + period, :], preferred_element_type=jnp.float32
            )
        raw_re, raw_im = raw[:NB], raw[NB:]
        seg = seg_at(i)
        own[seg, :NB, :] = ((resp_re * raw_re - resp_im * raw_im) * alive).astype(jnp.bfloat16)
        own[seg, NB:, :] = ((resp_re * raw_im + resp_im * raw_re) * alive).astype(jnp.bfloat16)
        if i == 0:
            pl.semaphore_wait(barrier, 5)
        start(own.at[seg], own.at[seg], recv_x.at[i], (me, other))
        spread(i)
    fetches[-1].wait()

    squares_own = jnp.zeros((channels, NB), jnp.float32)
    puts = []

    def put_out(src, dst):
        copy = pltpu.make_async_copy(src, dst, put.at[len(puts)])
        copy.start()
        puts.append(copy)

    def turn(i, total):
        seg = seg_at(i)
        re = own[seg, :NB, :].astype(jnp.float32).T
        im = own[seg, NB:, :].astype(jnp.float32).T

        def one_lag(l, carry):
            pair = lag_table[l]
            cos, sin = pair[0:1], pair[1:2]
            rows = pl.ds(pl.multiple_of(l * channels, channels), channels)
            turned[seg, rows, :NB] = (re * cos - im * sin).astype(jnp.bfloat16)
            turned[seg, rows, NB:] = (re * sin + im * cos).astype(jnp.bfloat16)
            return carry

        lax.fori_loop(0, lag_count, one_lag, 0)
        put_out(turned.at[seg], turned_out.at[seg])
        return total + (re * re + im * im)

    for i in range(2 * segs):
        if i < segs:
            arrived(own.at[seg_at(segs + i)], recv_x.at[i])
            spread(segs + i)
        hand_on(1, i)
        relay(i)
        if i:
            hand_on(4, i - 1)
        squares_own = turn(i, squares_own)
    own_mean = jnp.sum(squares_own, axis=1, keepdims=True) / (SEG * NB)
    own_scale[...] = jnp.broadcast_to(
        lax.rsqrt(own_mean + 1e-06) * (1.0 / math.sqrt(SEG * NB)), own_scale.shape
    )
    put_out(own_scale, scale_out)
    hand_on(4, 2 * segs - 1)
    for role in (0, 5):
        for i in range(2 * segs):
            wait_win(role, seg_at(i))
    for copy, only in sends:
        if only is None:
            copy.wait_send()
        else:
            pl.when(only)(copy.wait_send)
    for copy in puts:
        copy.wait()


def correlate_kernel(count, place, partners, turned, win, own_scale, out, factor):
    me = place[0]
    core = lax.rem(me, 2)
    side = lax.rem(me // 2, 2)
    offsets = (1 - 2 * core, 2 - 4 * side, -4, 4, 4 * side - 2, 2 * core - 1)
    channels = win.shape[3]

    @pl.when(pl.program_id(0) == 0)
    def _():
        for role in range(ROLES):
            total = jnp.zeros((8, channels), jnp.float32)
            for seg in range(SEG):
                rows = win[role, seg].astype(jnp.float32)
                total += jnp.sum((rows * rows).reshape(-1, 8, channels), axis=0)
            mean = jnp.sum(total, axis=0, keepdims=True) / (SEG * NB)
            factor[role] = own_scale[...] * lax.rsqrt(mean + 1e-06)

    def role_of(r):
        delta = lax.rem(partners[r] - me + count + count // 2, count) - count // 2
        role = jnp.int32(0)
        for position, offset in enumerate(offsets):
            role = role + jnp.where(delta == offset, position, 0)
        return role

    left = jnp.concatenate([turned[seg] for seg in range(SEG)], axis=1)
    for r in range(0, ROUNDS, 2):
        roles = (role_of(r), role_of(r + 1))
        chosen = jnp.concatenate([win[role].reshape(-1, channels) for role in roles], axis=1)
        sums = jnp.dot(left, chosen, preferred_element_type=jnp.float32)
        for k in range(2):
            part = sums[:, k * channels:(k + 1) * channels].reshape(GROUP, channels, channels)
            out[r + k] = part * factor[roles[k]][None]


def local(records, band_taps, white_taps, live_mask, partners):
    segs, samples, channels = records.shape
    count = lax.axis_size("chan")
    lag_count = LAGS // lax.axis_size("tm")
    bins = bin_numbers(samples)
    period = samples // math.gcd(samples, math.gcd(int(bins[0]), int(bins[1] - bins[0])))
    cos, sin = rotation(bins[:, None] * np.arange(period)[None, :], samples)
    table = np.concatenate([cos, -sin], axis=0).astype(np.float32).astype(jnp.bfloat16)
    band_table = np.concatenate(rotation(bins[:, None] * np.arange(band_taps.shape[0])[None, :], samples), axis=1)
    white_table = np.concatenate(rotation(bins[:, None] * np.arange(white_taps.shape[0])[None, :], samples), axis=0)
    lags = 3 * (np.arange(LAGS) - LAGS // 2)
    lag_table = np.stack(rotation(lags[:, None] * bins[None, :], samples), axis=1)
    f32 = lambda a: jnp.asarray(a.astype(np.float32))
    operands = (
        records, jnp.asarray(table), f32(band_table), f32(white_table), f32(lag_table),
        band_taps.reshape(1, -1), white_taps, live_mask.reshape(1, -1),
    )

    hbm = pl.BlockSpec(memory_space=pltpu.HBM)
    smem = pl.BlockSpec(memory_space=SMEM)
    win, turned, own_scale = pl.pallas_call(
        functools.partial(gather_kernel, count, segs),
        out_shape=(
            jax.ShapeDtypeStruct((ROLES, SEG, 2 * NB, channels), jnp.bfloat16),
            jax.ShapeDtypeStruct((SEG, lag_count * channels, 2 * NB), jnp.bfloat16),
            jax.ShapeDtypeStruct((channels, channels), jnp.float32),
        ),
        in_specs=[hbm] * len(operands),
        out_specs=(hbm, hbm, hbm),
        scratch_shapes=[
            VMEM((SEG, 2 * NB, channels), jnp.bfloat16),
            VMEM((SEG, lag_count * channels, 2 * NB), jnp.bfloat16),
            VMEM((channels, channels), jnp.float32),
            VMEM(records.shape, jnp.bfloat16),
            VMEM(table.shape, jnp.bfloat16),
            VMEM(band_table.shape, jnp.float32),
            VMEM(white_table.shape, jnp.float32),
            VMEM((lag_count, 2, NB), jnp.float32),
            VMEM((1, band_taps.shape[0]), jnp.float32),
            VMEM(white_taps.shape, jnp.float32),
            VMEM((1, channels), jnp.int32),
            pltpu.SemaphoreType.DMA((7 + segs,)),
            pltpu.SemaphoreType.DMA((segs + 8 * SEG,)),
            pltpu.SemaphoreType.DMA((segs,)),
            pltpu.SemaphoreType.DMA((ROLES, SEG)),
            pltpu.SemaphoreType.DMA((SEG + 1,)),
        ],
        compiler_params=pltpu.CompilerParams(
            collective_id=0, has_side_effects=True, vmem_limit_bytes=WHOLE_VMEM
        ),
        name="spectra_gather",
    )(*operands)

    place = lax.axis_index("chan").astype(jnp.int32).reshape(1)
    return pl.pallas_call(
        functools.partial(correlate_kernel, count),
        grid=(lag_count // GROUP,),
        out_shape=jax.ShapeDtypeStruct((ROUNDS, lag_count, channels, channels), jnp.float32),
        in_specs=[
            smem, smem,
            pl.BlockSpec((SEG, GROUP * channels, 2 * NB), lambda i: (0, i, 0)),
            pl.BlockSpec(win.shape, lambda i: (0, 0, 0, 0)),
            pl.BlockSpec(own_scale.shape, lambda i: (0, 0)),
        ],
        out_specs=pl.BlockSpec((ROUNDS, GROUP, channels, channels), lambda i: (0, i, 0, 0)),
        scratch_shapes=[VMEM((ROLES, channels, channels), jnp.float32)],
        compiler_params=pltpu.CompilerParams(vmem_limit_bytes=WHOLE_VMEM),
        name="correlate",
    )(place, partners.reshape(-1), turned, win, own_scale)


def solution(mesh):
    return jax.shard_map(
        local,
        mesh=mesh,
        in_specs=(P("tm", None, "chan"), P(), P(None, "chan"), P("chan"), P(None, "chan")),
        out_specs=P(None, "tm", "chan", None),
        check_vma=False,
    )
```

```python
import functools
import math

import jax
import jax.numpy as jnp
import numpy as np
from jax import lax
from jax.experimental import pallas as pl
from jax.experimental.pallas import tpu as pltpu
from jax.sharding import PartitionSpec as P

NB = 128
SEG = 6
LAGS = 32
ROUNDS = 6
GROUP = 8
MESH = pl.DeviceIdType.MESH
VMEM = pltpu.VMEM
SMEM = pltpu.SMEM
ROLES = 6
WHOLE_VMEM = 63_480_000


def bin_numbers(samples):
    return samples // 64 + samples // (4 * NB) * np.arange(NB, dtype=np.int64)


def rotation(products, samples):
    angles = np.mod(products, samples) * (2.0 * math.pi / samples)
    return np.cos(angles), np.sin(angles)


def gather_kernel(
    count, segs,
    rec_in, table_in, band_table_in, white_table_in, lag_table_in, band_in, white_in, live_in,
    partners, out,
    own, win_a, win_b, turned_a, turned_b, staged, win_scale, rec, table, band_table, white_table, lag_table, band, white, live,
    fetch, send, recv_x, recv_w, put,
):
    me = lax.axis_index("chan")
    tm = lax.axis_index("tm")
    core = lax.rem(me, 2)
    side = lax.rem(me // 2, 2)
    up = lax.rem(me + 4, count)
    down = lax.rem(me + count - 4, count)
    sib = me + 1 - 2 * core
    across = me + 2 - 4 * side
    other = 1 - tm
    lag_count, channels = lag_table.shape[0], own.shape[2]

    barrier = pltpu.get_barrier_semaphore()
    for peer in ((me, other), (up, tm), (down, tm), (across, tm), (sib, tm)):
        pl.semaphore_signal(barrier, inc=1, device_id=peer, device_id_type=MESH)

    pairs = [(band_in, band), (white_in, white), (live_in, live), (band_table_in, band_table),
             (white_table_in, white_table), (table_in, table)]
    pairs += [(rec_in.at[i], rec.at[i]) for i in range(segs)]
    pairs += [(lag_table_in.at[pl.ds(tm * lag_count, lag_count)], lag_table)]
    fetches = [pltpu.make_async_copy(src, dst, fetch.at[i]) for i, (src, dst) in enumerate(pairs)]
    for copy in fetches:
        copy.start()

    def win_at(role, i):
        return win_a.at[role, i] if i < segs else win_b.at[role, i - segs]

    sends = []

    def start(src, dst, sem, peer, only=None):
        copy = pltpu.make_async_remote_copy(
            src_ref=src, dst_ref=dst, send_sem=send.at[len(sends)], recv_sem=sem,
            device_id=peer, device_id_type=MESH,
        )
        sends.append((copy, only))
        if only is None:
            copy.start()
        else:
            pl.when(only)(copy.start)

    def arrived(dst, sem):
        pltpu.make_async_remote_copy(
            src_ref=dst, dst_ref=dst, send_sem=send.at[0], recv_sem=sem,
            device_id=(me, other), device_id_type=MESH,
        ).wait_recv()

    def wait_win(role, i):
        arrived(win_at(role, i), recv_w.at[role, i])

    first_row, last_row = me < 4, me >= count - 4
    mixed = lax.rem(core + side, 2)
    relay_src = 3 - side
    beyond = jnp.where(first_row, 2, 3)

    def send_win(src, role, i, peer, only=None):
        start(src, win_at(role, i), recv_w.at[role, i], peer, only)

    def spread(i):
        second = i >= segs
        send_win(own.at[i], 2, i, (up, tm), jnp.logical_not(last_row) if second else None)
        send_win(own.at[i], 3, i, (down, tm), jnp.logical_not(first_row) if second else None)
        if not second:
            send_win(own.at[i], 1, i, (across, tm))
        send_win(own.at[i], 0, i, (sib, tm))

    def relay(i):
        wait_win(relay_src, i)
        send_win(win_at(relay_src, i), 4, i, (across, tm))
        wait_win(2 + side, i)
        if i < segs:
            send_win(win_at(beyond, i), beyond, segs + i, (me, other), jnp.logical_or(first_row, last_row))

    def hand_on(role, i):
        wait_win(role, i)
        if role == 1 and i < segs:
            send_win(win_at(1, i), 1, segs + i, (me, other))
        send_win(win_at(role, i), 5, i, (sib, tm), mixed == role // 4)

    for copy in fetches[:5]:
        copy.wait()
    taps, band_count = band[...], band.shape[1]
    band_re = jnp.sum(band_table[:, :band_count] * taps, axis=1, keepdims=True)
    band_im = -jnp.sum(band_table[:, band_count:] * taps, axis=1, keepdims=True)
    white_resp = jnp.dot(
        white_table[...], white[...], precision=lax.Precision.HIGHEST, preferred_element_type=jnp.float32
    )
    white_re, white_im = white_resp[:NB], -white_resp[NB:]
    alive = live[...].astype(jnp.float32)
    resp_re = white_re * band_re - white_im * band_im
    resp_im = white_re * band_im + white_im * band_re

    period = table.shape[1]
    fetches[5].wait()
    for i in range(segs):
        fetches[6 + i].wait()
        raw = jnp.zeros((2 * NB, channels), jnp.float32)
        for first in range(0, rec.shape[1], period):
            raw = raw + jnp.dot(
                table[...], rec[i, first:first + period, :], preferred_element_type=jnp.float32
            )
        raw_re, raw_im = raw[:NB], raw[NB:]
        own[i, :NB, :] = ((resp_re * raw_re - resp_im * raw_im) * alive).astype(jnp.bfloat16)
        own[i, NB:, :] = ((resp_re * raw_im + resp_im * raw_re) * alive).astype(jnp.bfloat16)
        if i == 0:
            pl.semaphore_wait(barrier, 5)
        start(own.at[i], own.at[segs + i], recv_x.at[i], (me, other))
        spread(i)
    fetches[-1].wait()

    squares_own = jnp.zeros((channels, NB), jnp.float32)
    puts = []

    def turn(i, total):
        re = own[i, :NB, :].astype(jnp.float32).T
        im = own[i, NB:, :].astype(jnp.float32).T
        turned = turned_a if i < segs else turned_b
        at = (i % segs) * 2 * NB

        def one_lag(l, carry):
            pair = lag_table[l]
            cos, sin = pair[0:1], pair[1:2]
            rows = pl.ds(pl.multiple_of(l * channels, channels), channels)
            turned[rows, at:at + NB] = (re * cos - im * sin).astype(jnp.bfloat16)
            turned[rows, at + NB:at + 2 * NB] = (re * sin + im * cos).astype(jnp.bfloat16)
            return carry

        lax.fori_loop(0, lag_count, one_lag, 0)
        return total + (re * re + im * im)

    def add_squares(totals, win):
        totals = list(totals)
        for role in range(ROLES):
            for i in range(segs):
                rows = win[role, i].astype(jnp.float32)
                totals[role] += jnp.sum((rows * rows).reshape(-1, 8, channels), axis=0)
        return totals

    offsets = (1 - 2 * core, 2 - 4 * side, -4, 4, 4 * side - 2, 2 * core - 1)
    roles = []
    for r in range(ROUNDS):
        delta = lax.rem(partners[r] - me + count + count // 2, count) - count // 2
        role = jnp.int32(0)
        for position, offset in enumerate(offsets):
            role = role + jnp.where(delta == offset, position, 0)
        roles.append(role)

    def multiply(r, turned, win, factor=None):
        for g in range(lag_count // GROUP):
            lags = pl.ds(g * GROUP, GROUP)
            rows = pl.ds(g * GROUP * channels, GROUP * channels)
            chosen = jnp.concatenate([win[roles[r + k]].reshape(-1, channels) for k in range(2)], axis=1)
            sums = jnp.dot(turned[rows, :], chosen, preferred_element_type=jnp.float32)
            sums = sums.reshape(GROUP, channels, 2 * channels)
            for k in range(2):
                mine = slice(k * channels, (k + 1) * channels)
                if factor is None:
                    staged[r + k, lags] = sums[:, :, mine]
                else:
                    staged[r + k, lags] = (staged[r + k, lags] + sums[:, :, mine]) * factor[k][None]
                    copy = pltpu.make_async_copy(
                        staged.at[r + k, lags], out.at[r + k, lags], put.at[len(puts)]
                    )
                    copy.start()
                    puts.append(copy)

    squares_win = [jnp.zeros((8, channels), jnp.float32)] * ROLES
    for i in range(segs):
        arrived(own.at[segs + i], recv_x.at[i])
        spread(segs + i)
        hand_on(1, i)
        relay(i)
        if i:
            hand_on(4, i - 1)
        squares_own = turn(i, squares_own)
    for i in range(segs, 2 * segs):
        hand_on(1, i)
        relay(i)
        hand_on(4, i - 1)
        if i == segs:
            squares_own = turn(segs, squares_own)
            squares_own = turn(segs + 1, squares_own)
        if i == segs + 1:
            squares_own = turn(segs + 2, squares_own)
            for role in (0, 5):
                for j in range(segs):
                    wait_win(role, j)
            multiply(0, turned_a, win_a)
    multiply(2, turned_a, win_a)
    squares_win = add_squares(squares_win, win_a)
    hand_on(4, 2 * segs - 1)
    multiply(4, turned_a, win_a)
    own_mean = jnp.sum(squares_own, axis=1, keepdims=True) / (SEG * NB)
    own_scale = lax.rsqrt(own_mean + 1e-06) * (1.0 / math.sqrt(SEG * NB))
    for role in (0, 5):
        for i in range(segs, 2 * segs):
            wait_win(role, i)
    squares_win = add_squares(squares_win, win_b)
    for role in range(ROLES):
        mean = jnp.sum(squares_win[role], axis=0, keepdims=True) / (SEG * NB)
        win_scale[role] = lax.rsqrt(mean + 1e-06)
    for r in range(0, ROUNDS, 2):
        factor = [own_scale * win_scale[roles[r + k]] for k in range(2)]
        multiply(r, turned_b, win_b, factor)
    for copy, only in sends:
        if only is None:
            copy.wait_send()
        else:
            pl.when(only)(copy.wait_send)
    for copy in puts:
        copy.wait()


def local(records, band_taps, white_taps, live_mask, partners):
    segs, samples, channels = records.shape
    count = lax.axis_size("chan")
    lag_count = LAGS // lax.axis_size("tm")
    bins = bin_numbers(samples)
    period = samples // math.gcd(samples, math.gcd(int(bins[0]), int(bins[1] - bins[0])))
    cos, sin = rotation(bins[:, None] * np.arange(period)[None, :], samples)
    table = np.concatenate([cos, -sin], axis=0).astype(np.float32).astype(jnp.bfloat16)
    band_table = np.concatenate(rotation(bins[:, None] * np.arange(band_taps.shape[0])[None, :], samples), axis=1)
    white_table = np.concatenate(rotation(bins[:, None] * np.arange(white_taps.shape[0])[None, :], samples), axis=0)
    lags = 3 * (np.arange(LAGS) - LAGS // 2)
    lag_table = np.stack(rotation(lags[:, None] * bins[None, :], samples), axis=1)
    f32 = lambda a: jnp.asarray(a.astype(np.float32))
    operands = (
        records, jnp.asarray(table), f32(band_table), f32(white_table), f32(lag_table),
        band_taps.reshape(1, -1), white_taps, live_mask.reshape(1, -1),
    )

    hbm = pl.BlockSpec(memory_space=pltpu.HBM)
    smem = pl.BlockSpec(memory_space=SMEM)
    half = segs * 2 * NB
    shape = (ROUNDS, lag_count, channels, channels)
    return pl.pallas_call(
        functools.partial(gather_kernel, count, segs),
        out_shape=jax.ShapeDtypeStruct(shape, jnp.float32),
        in_specs=[hbm] * len(operands) + [smem],
        out_specs=hbm,
        scratch_shapes=[
            VMEM((SEG, 2 * NB, channels), jnp.bfloat16),
            VMEM((ROLES, segs, 2 * NB, channels), jnp.bfloat16),
            VMEM((ROLES, segs, 2 * NB, channels), jnp.bfloat16),
            VMEM((lag_count * channels, half), jnp.bfloat16),
            VMEM((lag_count * channels, half), jnp.bfloat16),
            VMEM(shape, jnp.float32),
            VMEM((ROLES, 1, channels), jnp.float32),
            VMEM(records.shape, jnp.bfloat16),
            VMEM(table.shape, jnp.bfloat16),
            VMEM(band_table.shape, jnp.float32),
            VMEM(white_table.shape, jnp.float32),
            VMEM((lag_count, 2, NB), jnp.float32),
            VMEM((1, band_taps.shape[0]), jnp.float32),
            VMEM(white_taps.shape, jnp.float32),
            VMEM((1, channels), jnp.int32),
            pltpu.SemaphoreType.DMA((7 + segs,)),
            pltpu.SemaphoreType.DMA((segs + 8 * SEG,)),
            pltpu.SemaphoreType.DMA((segs,)),
            pltpu.SemaphoreType.DMA((ROLES, SEG)),
            pltpu.SemaphoreType.DMA((ROUNDS * lag_count // GROUP,)),
        ],
        compiler_params=pltpu.CompilerParams(
            collective_id=0, has_side_effects=True, vmem_limit_bytes=WHOLE_VMEM
        ),
        name="correlations",
    )(*operands, partners.reshape(-1))


def solution(mesh):
    return jax.shard_map(
        local,
        mesh=mesh,
        in_specs=(P("tm", None, "chan"), P(), P(None, "chan"), P("chan"), P(None, "chan")),
        out_specs=P(None, "tm", "chan", None),
        check_vma=False,
    )
```

```python
import functools
import math

import jax
import jax.numpy as jnp
import numpy as np
from jax import lax
from jax.experimental import pallas as pl
from jax.experimental.pallas import tpu as pltpu
from jax.sharding import PartitionSpec as P

NB = 128
SEG = 6
LAGS = 32
ROUNDS = 6
GROUP = 4
MESH = pl.DeviceIdType.MESH
VMEM = pltpu.VMEM
SMEM = pltpu.SMEM
ROLES = 6
WHOLE_VMEM = 63_480_000


def bin_numbers(samples):
    return samples // 64 + samples // (4 * NB) * np.arange(NB, dtype=np.int64)


def rotation(products, samples):
    angles = np.mod(products, samples) * (2.0 * math.pi / samples)
    return np.cos(angles), np.sin(angles)


def gather_kernel(
    count, segs,
    rec_in, table_in, band_table_in, white_table_in, band_in, white_in, live_in,
    win, own_out,
    own, own_t, rec, table, band_table, white_table, band, white, live,
    fetch, send, recv_x, recv_w, put,
):
    me = lax.axis_index("chan")
    tm = lax.axis_index("tm")
    core = lax.rem(me, 2)
    side = lax.rem(me // 2, 2)
    up = lax.rem(me + 4, count)
    down = lax.rem(me + count - 4, count)
    sib = me + 1 - 2 * core
    across = me + 2 - 4 * side
    other = 1 - tm
    channels = own.shape[2]

    barrier = pltpu.get_barrier_semaphore()
    for peer in ((me, other), (up, tm), (down, tm), (across, tm), (sib, tm)):
        pl.semaphore_signal(barrier, inc=1, device_id=peer, device_id_type=MESH)

    pairs = [(band_in, band), (white_in, white), (live_in, live), (band_table_in, band_table),
             (white_table_in, white_table), (table_in, table)]
    pairs += [(rec_in.at[i], rec.at[i]) for i in range(segs)]
    fetches = [pltpu.make_async_copy(src, dst, fetch.at[i]) for i, (src, dst) in enumerate(pairs)]
    for copy in fetches:
        copy.start()

    def seg_at(i):
        return tm * segs + i if i < segs else other * segs + (i - segs)

    sends = []

    def start(src, dst, sem, peer, only=None):
        copy = pltpu.make_async_remote_copy(
            src_ref=src, dst_ref=dst, send_sem=send.at[len(sends)], recv_sem=sem,
            device_id=peer, device_id_type=MESH,
        )
        sends.append((copy, only))
        if only is None:
            copy.start()
        else:
            pl.when(only)(copy.start)

    def arrived(dst, sem):
        pltpu.make_async_remote_copy(
            src_ref=dst, dst_ref=dst, send_sem=send.at[0], recv_sem=sem,
            device_id=(me, other), device_id_type=MESH,
        ).wait_recv()

    def wait_win(role, seg):
        arrived(win.at[role, seg], recv_w.at[role, seg])

    first_row, last_row = me < 4, me >= count - 4
    mixed = lax.rem(core + side, 2)
    relay_src = 3 - side
    beyond = jnp.where(first_row, 2, 3)

    def send_win(src, role, seg, peer, only=None):
        start(src, win.at[role, seg], recv_w.at[role, seg], peer, only)

    def spread(i):
        seg = seg_at(i)
        second = i >= segs
        send_win(own.at[seg], 2, seg, (up, tm), jnp.logical_not(last_row) if second else None)
        send_win(own.at[seg], 3, seg, (down, tm), jnp.logical_not(first_row) if second else None)
        if not second:
            send_win(own.at[seg], 1, seg, (across, tm))
        send_win(own.at[seg], 0, seg, (sib, tm))

    def relay(i):
        seg = seg_at(i)
        wait_win(relay_src, seg)
        send_win(win.at[relay_src, seg], 4, seg, (across, tm))
        wait_win(2 + side, seg)
        if i < segs:
            send_win(win.at[beyond, seg], beyond, seg, (me, other), jnp.logical_or(first_row, last_row))

    def hand_on(role, i):
        seg = seg_at(i)
        wait_win(role, seg)
        if role == 1 and i < segs:
            send_win(win.at[1, seg], 1, seg, (me, other))
        send_win(win.at[role, seg], 5, seg, (sib, tm), mixed == role // 4)

    for copy in fetches[:5]:
        copy.wait()
    taps, band_count = band[...], band.shape[1]
    band_re = jnp.sum(band_table[:, :band_count] * taps, axis=1, keepdims=True)
    band_im = -jnp.sum(band_table[:, band_count:] * taps, axis=1, keepdims=True)
    white_resp = jnp.dot(
        white_table[...], white[...], precision=lax.Precision.HIGHEST, preferred_element_type=jnp.float32
    )
    white_re, white_im = white_resp[:NB], -white_resp[NB:]
    alive = live[...].astype(jnp.float32)
    resp_re = white_re * band_re - white_im * band_im
    resp_im = white_re * band_im + white_im * band_re

    period = table.shape[1]
    fetches[5].wait()
    for i in range(segs):
        fetches[6 + i].wait()
        raw = jnp.zeros((2 * NB, channels), jnp.float32)
        for first in range(0, rec.shape[1], period):
            raw = raw + jnp.dot(
                table[...], rec[i, first:first + period, :], preferred_element_type=jnp.float32
            )
        raw_re, raw_im = raw[:NB], raw[NB:]
        seg = seg_at(i)
        own[seg, :NB, :] = ((resp_re * raw_re - resp_im * raw_im) * alive).astype(jnp.bfloat16)
        own[seg, NB:, :] = ((resp_re * raw_im + resp_im * raw_re) * alive).astype(jnp.bfloat16)
        if i == 0:
            pl.semaphore_wait(barrier, 5)
        start(own.at[seg], own.at[seg], recv_x.at[i], (me, other))
        spread(i)

    def transpose(i):
        seg = seg_at(i)
        for part in (slice(0, NB), slice(NB, 2 * NB)):
            own_t[seg, :, part] = own[seg, part, :].astype(jnp.float32).T.astype(jnp.bfloat16)

    for i in range(2 * segs):
        if i < segs:
            arrived(own.at[seg_at(segs + i)], recv_x.at[i])
            spread(segs + i)
        hand_on(1, i)
        relay(i)
        if i:
            hand_on(4, i - 1)
        if i >= segs:
            transpose(i - segs)
            transpose(i)
    put_out = pltpu.make_async_copy(own_t, own_out, put)
    put_out.start()
    hand_on(4, 2 * segs - 1)
    for role in (0, 5):
        for i in range(2 * segs):
            wait_win(role, seg_at(i))
    for copy, only in sends:
        if only is None:
            copy.wait_send()
        else:
            pl.when(only)(copy.wait_send)
    put_out.wait()


def correlate_kernel(
    count, place, partners, own_in, lag_in, win_in, out,
    own, lag_table, wide, turned_even, turned_odd, staged, chosen, get, put,
):
    me = place[0]
    core = lax.rem(me, 2)
    side = lax.rem(me // 2, 2)
    offsets = (1 - 2 * core, 2 - 4 * side, -4, 4, 4 * side - 2, 2 * core - 1)
    lag_count, channels = lag_table.shape[0], own.shape[1]
    groups = lag_count // GROUP

    gets = [
        pltpu.make_async_copy(own_in, own, get.at[ROUNDS]),
        pltpu.make_async_copy(lag_in.at[pl.ds(place[1] * lag_count, lag_count)], lag_table, get.at[ROUNDS + 1]),
    ]
    for r in range(ROUNDS):
        delta = lax.rem(partners[r] - me + count + count // 2, count) - count // 2
        role = jnp.int32(0)
        for position, offset in enumerate(offsets):
            role = role + jnp.where(delta == offset, position, 0)
        gets.append(pltpu.make_async_copy(win_in.at[role], chosen.at[r], get.at[r]))
    for copy in gets:
        copy.start()

    def turn(g, segments):
        turned = (turned_even, turned_odd)[g % 2]
        for l in range(GROUP):
            pair = lag_table[g * GROUP + l]
            cos, sin = pair[0:1], pair[1:2]
            rows = slice(l * channels, (l + 1) * channels)
            for seg in segments:
                at = 2 * seg * NB
                re, im = wide[seg, :, :NB], wide[seg, :, NB:]
                turned[rows, at:at + NB] = (re * cos - im * sin).astype(jnp.bfloat16)
                turned[rows, at + NB:at + 2 * NB] = (re * sin + im * cos).astype(jnp.bfloat16)

    gets[0].wait()
    gets[1].wait()
    total = jnp.zeros((channels, 2 * NB), jnp.float32)
    for seg in range(SEG):
        values = own[seg].astype(jnp.float32)
        wide[seg] = values
        total += values * values
    own_mean = jnp.sum(total, axis=1, keepdims=True) / (SEG * NB)
    own_scale = lax.rsqrt(own_mean + 1e-06) * (1.0 / math.sqrt(SEG * NB))
    turn(0, range(SEG))

    scales = []
    for r in range(ROUNDS):
        gets[2 + r].wait()
        squares = jnp.zeros((8, channels), jnp.float32)
        for seg in range(SEG):
            rows = chosen[r, seg].astype(jnp.float32)
            squares += jnp.sum((rows * rows).reshape(-1, 8, channels), axis=0)
        mean = jnp.sum(squares, axis=0, keepdims=True) / (SEG * NB)
        scales.append(own_scale * lax.rsqrt(mean + 1e-06))

    puts = []
    for g in range(groups):
        turned = (turned_even, turned_odd)[g % 2]
        lags = pl.ds(g * GROUP, GROUP)
        for r in range(0, ROUNDS, 2):
            right = jnp.concatenate([chosen[r + k].reshape(-1, channels) for k in range(2)], axis=1)
            sums = jnp.dot(turned[...], right, preferred_element_type=jnp.float32)
            if g + 1 < groups:
                turn(g + 1, (r, r + 1))
            for k in range(2):
                part = sums[:, k * channels:(k + 1) * channels].reshape(GROUP, channels, channels)
                staged[r + k, lags] = part * scales[r + k][None]
                copy = pltpu.make_async_copy(staged.at[r + k, lags], out.at[r + k, lags], put.at[len(puts)])
                copy.start()
                puts.append(copy)
    for copy in puts:
        copy.wait()


def local(records, band_taps, white_taps, live_mask, partners):
    segs, samples, channels = records.shape
    count = lax.axis_size("chan")
    lag_count = LAGS // lax.axis_size("tm")
    bins = bin_numbers(samples)
    period = samples // math.gcd(samples, math.gcd(int(bins[0]), int(bins[1] - bins[0])))
    cos, sin = rotation(bins[:, None] * np.arange(period)[None, :], samples)
    table = np.concatenate([cos, -sin], axis=0).astype(np.float32).astype(jnp.bfloat16)
    band_table = np.concatenate(rotation(bins[:, None] * np.arange(band_taps.shape[0])[None, :], samples), axis=1)
    white_table = np.concatenate(rotation(bins[:, None] * np.arange(white_taps.shape[0])[None, :], samples), axis=0)
    lags = 3 * (np.arange(LAGS) - LAGS // 2)
    lag_table = np.stack(rotation(lags[:, None] * bins[None, :], samples), axis=1)
    f32 = lambda a: jnp.asarray(a.astype(np.float32))
    operands = (
        records, jnp.asarray(table), f32(band_table), f32(white_table),
        band_taps.reshape(1, -1), white_taps, live_mask.reshape(1, -1),
    )

    hbm = pl.BlockSpec(memory_space=pltpu.HBM)
    smem = pl.BlockSpec(memory_space=SMEM)
    win, own_t = pl.pallas_call(
        functools.partial(gather_kernel, count, segs),
        out_shape=(
            jax.ShapeDtypeStruct((ROLES, SEG, 2 * NB, channels), jnp.bfloat16),
            jax.ShapeDtypeStruct((SEG, channels, 2 * NB), jnp.bfloat16),
        ),
        in_specs=[hbm] * len(operands),
        out_specs=(hbm, hbm),
        scratch_shapes=[
            VMEM((SEG, 2 * NB, channels), jnp.bfloat16),
            VMEM((SEG, channels, 2 * NB), jnp.bfloat16),
            VMEM(records.shape, jnp.bfloat16),
            VMEM(table.shape, jnp.bfloat16),
            VMEM(band_table.shape, jnp.float32),
            VMEM(white_table.shape, jnp.float32),
            VMEM((1, band_taps.shape[0]), jnp.float32),
            VMEM(white_taps.shape, jnp.float32),
            VMEM((1, channels), jnp.int32),
            pltpu.SemaphoreType.DMA((6 + segs,)),
            pltpu.SemaphoreType.DMA((segs + 8 * SEG,)),
            pltpu.SemaphoreType.DMA((segs,)),
            pltpu.SemaphoreType.DMA((ROLES, SEG)),
            pltpu.SemaphoreType.DMA,
        ],
        compiler_params=pltpu.CompilerParams(
            collective_id=0, has_side_effects=True, vmem_limit_bytes=WHOLE_VMEM
        ),
        name="spectra_gather",
    )(*operands)

    place = jnp.stack([lax.axis_index("chan"), lax.axis_index("tm")]).astype(jnp.int32)
    shape = (ROUNDS, lag_count, channels, channels)
    inner = SEG * 2 * NB
    return pl.pallas_call(
        functools.partial(correlate_kernel, count),
        out_shape=jax.ShapeDtypeStruct(shape, jnp.float32),
        in_specs=[smem, smem, hbm, hbm, hbm],
        out_specs=hbm,
        scratch_shapes=[
            VMEM((SEG, channels, 2 * NB), jnp.bfloat16),
            VMEM((lag_count, 2, NB), jnp.float32),
            VMEM((SEG, channels, 2 * NB), jnp.float32),
            VMEM((GROUP * channels, inner), jnp.bfloat16),
            VMEM((GROUP * channels, inner), jnp.bfloat16),
            VMEM(shape, jnp.float32),
            VMEM((ROUNDS, SEG, 2 * NB, channels), jnp.bfloat16),
            pltpu.SemaphoreType.DMA((ROUNDS + 2,)),
            pltpu.SemaphoreType.DMA((ROUNDS * lag_count // GROUP,)),
        ],
        compiler_params=pltpu.CompilerParams(vmem_limit_bytes=WHOLE_VMEM),
        name="correlate",
    )(place, partners.reshape(-1), own_t, f32(lag_table), win)


def solution(mesh):
    return jax.shard_map(
        local,
        mesh=mesh,
        in_specs=(P("tm", None, "chan"), P(), P(None, "chan"), P("chan"), P(None, "chan")),
        out_specs=P(None, "tm", "chan", None),
        check_vma=False,
    )
```

```python
import functools
import math

import jax
import jax.numpy as jnp
import numpy as np
from jax import lax
from jax.experimental import pallas as pl
from jax.experimental.pallas import tpu as pltpu
from jax.sharding import PartitionSpec as P

NB = 128
SEG = 6
LAGS = 32
ROUNDS = 6
GROUP = 4
MESH = pl.DeviceIdType.MESH
VMEM = pltpu.VMEM
SMEM = pltpu.SMEM
ROLES = 6
WHOLE_VMEM = 63_480_000


def bin_numbers(samples):
    return samples // 64 + samples // (4 * NB) * np.arange(NB, dtype=np.int64)


def rotation(products, samples):
    angles = np.mod(products, samples) * (2.0 * math.pi / samples)
    return np.cos(angles), np.sin(angles)


def gather_kernel(
    count, segs,
    rec_in, table_in, band_table_in, white_table_in, lag_table_in, band_in, white_in, live_in,
    win, turned_out, scale_out,
    own, turned, own_scale, rec, table, band_table, white_table, lag_table, band, white, live,
    fetch, send, recv_x, recv_w, put,
):
    me = lax.axis_index("chan")
    tm = lax.axis_index("tm")
    core = lax.rem(me, 2)
    side = lax.rem(me // 2, 2)
    up = lax.rem(me + 4, count)
    down = lax.rem(me + count - 4, count)
    sib = me + 1 - 2 * core
    across = me + 2 - 4 * side
    other = 1 - tm
    lag_count, channels = lag_table.shape[0], own.shape[2]

    barrier = pltpu.get_barrier_semaphore()
    for peer in ((me, other), (up, tm), (down, tm), (across, tm), (sib, tm)):
        pl.semaphore_signal(barrier, inc=1, device_id=peer, device_id_type=MESH)

    pairs = [(band_in, band), (white_in, white), (live_in, live), (band_table_in, band_table),
             (white_table_in, white_table), (table_in, table)]
    pairs += [(rec_in.at[i], rec.at[i]) for i in range(segs)]
    pairs += [(lag_table_in.at[pl.ds(tm * lag_count, lag_count)], lag_table)]
    fetches = [pltpu.make_async_copy(src, dst, fetch.at[i]) for i, (src, dst) in enumerate(pairs)]
    for copy in fetches:
        copy.start()

    def seg_at(i):
        return tm * segs + i if i < segs else other * segs + (i - segs)

    sends = []

    def start(src, dst, sem, peer, only=None):
        copy = pltpu.make_async_remote_copy(
            src_ref=src, dst_ref=dst, send_sem=send.at[len(sends)], recv_sem=sem,
            device_id=peer, device_id_type=MESH,
        )
        sends.append((copy, only))
        if only is None:
            copy.start()
        else:
            pl.when(only)(copy.start)

    def arrived(dst, sem):
        pltpu.make_async_remote_copy(
            src_ref=dst, dst_ref=dst, send_sem=send.at[0], recv_sem=sem,
            device_id=(me, other), device_id_type=MESH,
        ).wait_recv()

    def wait_win(role, seg):
        arrived(win.at[role, seg], recv_w.at[role, seg])

    first_row, last_row = me < 4, me >= count - 4
    mixed = lax.rem(core + side, 2)
    relay_src = 3 - side
    beyond = jnp.where(first_row, 2, 3)

    def send_win(src, role, seg, peer, only=None):
        start(src, win.at[role, seg], recv_w.at[role, seg], peer, only)

    soon_peer, late_peer = jnp.where(side == 0, down, up), jnp.where(side == 0, up, down)
    soon_end = jnp.where(side == 0, me >= 4, me < count - 4)
    late_end = jnp.where(side == 0, me < count - 4, me >= 4)

    def spread(i):
        seg = seg_at(i)
        second = i >= segs
        send_win(own.at[seg], relay_src, seg, (soon_peer, tm), soon_end if second else None)
        if not second:
            send_win(own.at[seg], 1, seg, (across, tm))
        send_win(own.at[seg], 2 + side, seg, (late_peer, tm), late_end if second else None)
        send_win(own.at[seg], 0, seg, (sib, tm))

    def relay(i):
        seg = seg_at(i)
        wait_win(relay_src, seg)
        send_win(win.at[relay_src, seg], 4, seg, (across, tm))
        wait_win(2 + side, seg)
        if i < segs:
            send_win(win.at[beyond, seg], beyond, seg, (me, other), jnp.logical_or(first_row, last_row))

    def hand_on(role, i):
        seg = seg_at(i)
        wait_win(role, seg)
        if role == 1 and i < segs:
            send_win(win.at[1, seg], 1, seg, (me, other))
        send_win(win.at[role, seg], 5, seg, (sib, tm), mixed == role // 4)

    for copy in fetches[:5]:
        copy.wait()
    taps, band_count = band[...], band.shape[1]
    band_re = jnp.sum(band_table[:, :band_count] * taps, axis=1, keepdims=True)
    band_im = -jnp.sum(band_table[:, band_count:] * taps, axis=1, keepdims=True)
    white_resp = jnp.dot(
        white_table[...], white[...], precision=lax.Precision.HIGHEST, preferred_element_type=jnp.float32
    )
    white_re, white_im = white_resp[:NB], -white_resp[NB:]
    alive = live[...].astype(jnp.float32)
    resp_re = white_re * band_re - white_im * band_im
    resp_im = white_re * band_im + white_im * band_re

    period = table.shape[1]
    fetches[5].wait()
    for i in range(segs):
        fetches[6 + i].wait()
        raw = jnp.zeros((2 * NB, channels), jnp.float32)
        for first in range(0, rec.shape[1], period):
            raw = raw + jnp.dot(
                table[...], rec[i, first:first + period, :], preferred_element_type=jnp.float32
            )
        raw_re, raw_im = raw[:NB], raw[NB:]
        seg = seg_at(i)
        own[seg, :NB, :] = ((resp_re * raw_re - resp_im * raw_im) * alive).astype(jnp.bfloat16)
        own[seg, NB:, :] = ((resp_re * raw_im + resp_im * raw_re) * alive).astype(jnp.bfloat16)
        if i == 0:
            pl.semaphore_wait(barrier, 5)
        start(own.at[seg], own.at[seg], recv_x.at[i], (me, other))
        spread(i)
    fetches[-1].wait()

    squares_own = jnp.zeros((channels, NB), jnp.float32)
    puts = []

    def put_out(src, dst):
        copy = pltpu.make_async_copy(src, dst, put.at[len(puts)])
        copy.start()
        puts.append(copy)

    def turn(i, total):
        seg = seg_at(i)
        re = own[seg, :NB, :].astype(jnp.float32).T
        im = own[seg, NB:, :].astype(jnp.float32).T

        def one_lag(l, carry):
            pair = lag_table[l]
            cos, sin = pair[0:1], pair[1:2]
            rows = pl.ds(pl.multiple_of(l * channels, channels), channels)
            turned[seg, rows, :NB] = (re * cos - im * sin).astype(jnp.bfloat16)
            turned[seg, rows, NB:] = (re * sin + im * cos).astype(jnp.bfloat16)
            return carry

        lax.fori_loop(0, lag_count, one_lag, 0)
        put_out(turned.at[seg], turned_out.at[seg])
        return total + (re * re + im * im)

    for i in range(2 * segs):
        if i < segs:
            arrived(own.at[seg_at(segs + i)], recv_x.at[i])
            spread(segs + i)
        hand_on(1, i)
        relay(i)
        if i:
            hand_on(4, i - 1)
        squares_own = turn(i, squares_own)
    own_mean = jnp.sum(squares_own, axis=1, keepdims=True) / (SEG * NB)
    own_scale[...] = jnp.broadcast_to(
        lax.rsqrt(own_mean + 1e-06) * (1.0 / math.sqrt(SEG * NB)), own_scale.shape
    )
    put_out(own_scale, scale_out)
    hand_on(4, 2 * segs - 1)
    for role in (0, 5):
        for i in range(2 * segs):
            wait_win(role, seg_at(i))
    for copy, only in sends:
        if only is None:
            copy.wait_send()
        else:
            pl.when(only)(copy.wait_send)
    for copy in puts:
        copy.wait()


def correlate_kernel(
    count, place, partners, turned_in, win_in, scale_in, out,
    own_scale, turned, staged, chosen, get, get_turned, put,
):
    me = place[0]
    core = lax.rem(me, 2)
    side = lax.rem(me // 2, 2)
    offsets = (1 - 2 * core, 2 - 4 * side, -4, 4, 4 * side - 2, 2 * core - 1)
    channels = chosen.shape[3]
    groups = turned.shape[1] // (GROUP * channels)
    spans = [pl.ds(g * GROUP * channels, GROUP * channels) for g in range(groups)]

    gets = []
    for r in range(ROUNDS):
        delta = lax.rem(partners[r] - me + count + count // 2, count) - count // 2
        role = jnp.int32(0)
        for position, offset in enumerate(offsets):
            role = role + jnp.where(delta == offset, position, 0)
        gets.append(pltpu.make_async_copy(win_in.at[role], chosen.at[r], get.at[r]))
    gets.append(pltpu.make_async_copy(scale_in, own_scale, get.at[ROUNDS]))
    gets_turned = [
        pltpu.make_async_copy(turned_in.at[:, span], turned.at[:, span], get_turned.at[g])
        for g, span in enumerate(spans)
    ]
    for copy in (gets[0], gets[1], gets_turned[0], gets[ROUNDS], *gets[2:ROUNDS]):
        copy.start()

    def scale(r):
        squares = jnp.zeros((8, channels), jnp.float32)
        for seg in range(SEG):
            rows = chosen[r, seg].astype(jnp.float32)
            squares += jnp.sum((rows * rows).reshape(-1, 8, channels), axis=0)
        mean = jnp.sum(squares, axis=0, keepdims=True) / (SEG * NB)
        return own_scale[...] * lax.rsqrt(mean + 1e-06)

    scales, puts = [], []
    for g, span in enumerate(spans):
        lags = pl.ds(g * GROUP, GROUP)
        for r in range(0, ROUNDS, 2):
            if g == 0:
                gets[r].wait()
                gets[r + 1].wait()
                if r == 0:
                    gets[ROUNDS].wait()
            if r == 0:
                gets_turned[g].wait()
                for ahead in ((1, 2) if g == 0 else (g + 2,)):
                    if ahead < groups:
                        gets_turned[ahead].start()
            left = jnp.concatenate([turned[seg, span, :] for seg in range(SEG)], axis=1)
            right = jnp.concatenate([chosen[r + k].reshape(-1, channels) for k in range(2)], axis=1)
            sums = jnp.dot(left, right, preferred_element_type=jnp.float32)
            if g == 0:
                scales += [scale(r), scale(r + 1)]
            for k in range(2):
                part = sums[:, k * channels:(k + 1) * channels].reshape(GROUP, channels, channels)
                staged[r + k, lags] = part * scales[r + k][None]
                copy = pltpu.make_async_copy(staged.at[r + k, lags], out.at[r + k, lags], put.at[len(puts)])
                copy.start()
                puts.append(copy)
    for copy in puts:
        copy.wait()


def local(records, band_taps, white_taps, live_mask, partners):
    segs, samples, channels = records.shape
    count = lax.axis_size("chan")
    lag_count = LAGS // lax.axis_size("tm")
    bins = bin_numbers(samples)
    period = samples // math.gcd(samples, math.gcd(int(bins[0]), int(bins[1] - bins[0])))
    cos, sin = rotation(bins[:, None] * np.arange(period)[None, :], samples)
    table = np.concatenate([cos, -sin], axis=0).astype(np.float32).astype(jnp.bfloat16)
    band_table = np.concatenate(rotation(bins[:, None] * np.arange(band_taps.shape[0])[None, :], samples), axis=1)
    white_table = np.concatenate(rotation(bins[:, None] * np.arange(white_taps.shape[0])[None, :], samples), axis=0)
    lags = 3 * (np.arange(LAGS) - LAGS // 2)
    lag_table = np.stack(rotation(lags[:, None] * bins[None, :], samples), axis=1)
    f32 = lambda a: jnp.asarray(a.astype(np.float32))
    operands = (
        records, jnp.asarray(table), f32(band_table), f32(white_table), f32(lag_table),
        band_taps.reshape(1, -1), white_taps, live_mask.reshape(1, -1),
    )

    hbm = pl.BlockSpec(memory_space=pltpu.HBM)
    smem = pl.BlockSpec(memory_space=SMEM)
    win, turned, own_scale = pl.pallas_call(
        functools.partial(gather_kernel, count, segs),
        out_shape=(
            jax.ShapeDtypeStruct((ROLES, SEG, 2 * NB, channels), jnp.bfloat16),
            jax.ShapeDtypeStruct((SEG, lag_count * channels, 2 * NB), jnp.bfloat16),
            jax.ShapeDtypeStruct((channels, channels), jnp.float32),
        ),
        in_specs=[hbm] * len(operands),
        out_specs=(hbm, hbm, hbm),
        scratch_shapes=[
            VMEM((SEG, 2 * NB, channels), jnp.bfloat16),
            VMEM((SEG, lag_count * channels, 2 * NB), jnp.bfloat16),
            VMEM((channels, channels), jnp.float32),
            VMEM(records.shape, jnp.bfloat16),
            VMEM(table.shape, jnp.bfloat16),
            VMEM(band_table.shape, jnp.float32),
            VMEM(white_table.shape, jnp.float32),
            VMEM((lag_count, 2, NB), jnp.float32),
            VMEM((1, band_taps.shape[0]), jnp.float32),
            VMEM(white_taps.shape, jnp.float32),
            VMEM((1, channels), jnp.int32),
            pltpu.SemaphoreType.DMA((7 + segs,)),
            pltpu.SemaphoreType.DMA((segs + 8 * SEG,)),
            pltpu.SemaphoreType.DMA((segs,)),
            pltpu.SemaphoreType.DMA((ROLES, SEG)),
            pltpu.SemaphoreType.DMA((SEG + 1,)),
        ],
        compiler_params=pltpu.CompilerParams(
            collective_id=0, has_side_effects=True, vmem_limit_bytes=WHOLE_VMEM
        ),
        name="spectra_gather",
    )(*operands)

    place = lax.axis_index("chan").astype(jnp.int32).reshape(1)
    shape = (ROUNDS, lag_count, channels, channels)
    return pl.pallas_call(
        functools.partial(correlate_kernel, count),
        out_shape=jax.ShapeDtypeStruct(shape, jnp.float32),
        in_specs=[smem, smem, hbm, hbm, hbm],
        out_specs=hbm,
        scratch_shapes=[
            VMEM(own_scale.shape, jnp.float32),
            VMEM(turned.shape, jnp.bfloat16),
            VMEM(shape, jnp.float32),
            VMEM(win.shape, jnp.bfloat16),
            pltpu.SemaphoreType.DMA((ROUNDS + 1,)),
            pltpu.SemaphoreType.DMA((lag_count // GROUP,)),
            pltpu.SemaphoreType.DMA((ROUNDS * lag_count // GROUP,)),
        ],
        compiler_params=pltpu.CompilerParams(vmem_limit_bytes=WHOLE_VMEM),
        name="correlate",
    )(place, partners.reshape(-1), turned, win, own_scale)


def solution(mesh):
    return jax.shard_map(
        local,
        mesh=mesh,
        in_specs=(P("tm", None, "chan"), P(), P(None, "chan"), P("chan"), P(None, "chan")),
        out_specs=P(None, "tm", "chan", None),
        check_vma=False,
    )
```

```python
import functools
import math

import jax
import jax.numpy as jnp
import numpy as np
from jax import lax
from jax.experimental import pallas as pl
from jax.experimental.pallas import tpu as pltpu
from jax.sharding import PartitionSpec as P

NB = 128
SEG = 6
LAGS = 32
ROUNDS = 6
GROUP = 4
MESH = pl.DeviceIdType.MESH
VMEM = pltpu.VMEM
SMEM = pltpu.SMEM
ROLES = 6
WHOLE_VMEM = 63_480_000


def bin_numbers(samples):
    return samples // 64 + samples // (4 * NB) * np.arange(NB, dtype=np.int64)


def rotation(products, samples):
    angles = np.mod(products, samples) * (2.0 * math.pi / samples)
    return np.cos(angles), np.sin(angles)


def gather_kernel(
    count, segs,
    rec_in, table_in, band_table_in, white_table_in, band_in, white_in, live_in,
    win, own_out,
    own, own_t, rec, table, band_table, white_table, band, white, live,
    fetch, send, recv_x, recv_w, put,
):
    me = lax.axis_index("chan")
    tm = lax.axis_index("tm")
    core = lax.rem(me, 2)
    side = lax.rem(me // 2, 2)
    up = lax.rem(me + 4, count)
    down = lax.rem(me + count - 4, count)
    sib = me + 1 - 2 * core
    across = me + 2 - 4 * side
    other = 1 - tm
    channels = own.shape[2]

    barrier = pltpu.get_barrier_semaphore()
    for peer in ((me, other), (up, tm), (down, tm), (across, tm), (sib, tm)):
        pl.semaphore_signal(barrier, inc=1, device_id=peer, device_id_type=MESH)

    pairs = [(band_in, band), (white_in, white), (live_in, live), (band_table_in, band_table),
             (white_table_in, white_table), (table_in, table)]
    pairs += [(rec_in.at[i], rec.at[i]) for i in range(segs)]
    fetches = [pltpu.make_async_copy(src, dst, fetch.at[i]) for i, (src, dst) in enumerate(pairs)]
    for copy in fetches:
        copy.start()

    def seg_at(i):
        return tm * segs + i if i < segs else other * segs + (i - segs)

    sends = []

    def start(src, dst, sem, peer, only=None):
        copy = pltpu.make_async_remote_copy(
            src_ref=src, dst_ref=dst, send_sem=send.at[len(sends)], recv_sem=sem,
            device_id=peer, device_id_type=MESH,
        )
        sends.append((copy, only))
        if only is None:
            copy.start()
        else:
            pl.when(only)(copy.start)

    def arrived(dst, sem):
        pltpu.make_async_remote_copy(
            src_ref=dst, dst_ref=dst, send_sem=send.at[0], recv_sem=sem,
            device_id=(me, other), device_id_type=MESH,
        ).wait_recv()

    def wait_win(role, seg):
        arrived(win.at[role, seg], recv_w.at[role, seg])

    first_row, last_row = me < 4, me >= count - 4
    mixed = lax.rem(core + side, 2)
    relay_src = 3 - side
    beyond = jnp.where(first_row, 2, 3)

    def send_win(src, role, seg, peer, only=None):
        start(src, win.at[role, seg], recv_w.at[role, seg], peer, only)

    def spread(i):
        seg = seg_at(i)
        second = i >= segs
        send_win(own.at[seg], 2, seg, (up, tm), jnp.logical_not(last_row) if second else None)
        send_win(own.at[seg], 3, seg, (down, tm), jnp.logical_not(first_row) if second else None)
        if not second:
            send_win(own.at[seg], 1, seg, (across, tm))
        send_win(own.at[seg], 0, seg, (sib, tm))

    def relay(i):
        seg = seg_at(i)
        wait_win(relay_src, seg)
        send_win(win.at[relay_src, seg], 4, seg, (across, tm))
        wait_win(2 + side, seg)
        if i < segs:
            send_win(win.at[beyond, seg], beyond, seg, (me, other), jnp.logical_or(first_row, last_row))

    def hand_on(role, i):
        seg = seg_at(i)
        wait_win(role, seg)
        if role == 1 and i < segs:
            send_win(win.at[1, seg], 1, seg, (me, other))
        send_win(win.at[role, seg], 5, seg, (sib, tm), mixed == role // 4)

    for copy in fetches[:5]:
        copy.wait()
    taps, band_count = band[...], band.shape[1]
    band_re = jnp.sum(band_table[:, :band_count] * taps, axis=1, keepdims=True)
    band_im = -jnp.sum(band_table[:, band_count:] * taps, axis=1, keepdims=True)
    white_resp = jnp.dot(
        white_table[...], white[...], precision=lax.Precision.HIGHEST, preferred_element_type=jnp.float32
    )
    white_re, white_im = white_resp[:NB], -white_resp[NB:]
    alive = live[...].astype(jnp.float32)
    resp_re = white_re * band_re - white_im * band_im
    resp_im = white_re * band_im + white_im * band_re

    period = table.shape[1]
    fetches[5].wait()
    for i in range(segs):
        fetches[6 + i].wait()
        raw = jnp.zeros((2 * NB, channels), jnp.float32)
        for first in range(0, rec.shape[1], period):
            raw = raw + jnp.dot(
                table[...], rec[i, first:first + period, :], preferred_element_type=jnp.float32
            )
        raw_re, raw_im = raw[:NB], raw[NB:]
        seg = seg_at(i)
        own[seg, :NB, :] = ((resp_re * raw_re - resp_im * raw_im) * alive).astype(jnp.bfloat16)
        own[seg, NB:, :] = ((resp_re * raw_im + resp_im * raw_re) * alive).astype(jnp.bfloat16)
        if i == 0:
            pl.semaphore_wait(barrier, 5)
        start(own.at[seg], own.at[seg], recv_x.at[i], (me, other))
        spread(i)

    def transpose(i):
        seg = seg_at(i)
        for part in (slice(0, NB), slice(NB, 2 * NB)):
            own_t[seg, :, part] = own[seg, part, :].astype(jnp.float32).T.astype(jnp.bfloat16)

    for i in range(2 * segs):
        if i < segs:
            arrived(own.at[seg_at(segs + i)], recv_x.at[i])
            spread(segs + i)
        hand_on(1, i)
        relay(i)
        if i:
            hand_on(4, i - 1)
        if i >= segs:
            transpose(i - segs)
            transpose(i)
    put_out = pltpu.make_async_copy(own_t, own_out, put)
    put_out.start()
    hand_on(4, 2 * segs - 1)
    for role in (0, 5):
        for i in range(2 * segs):
            wait_win(role, seg_at(i))
    for copy, only in sends:
        if only is None:
            copy.wait_send()
        else:
            pl.when(only)(copy.wait_send)
    put_out.wait()


def correlate_kernel(
    count, chan_at, tm_at, partners, own_in, lag_in, win_in, out,
    own, lag_table, wide, turned_even, turned_odd, staged, chosen, get, put,
):
    me = chan_at[0]
    core = lax.rem(me, 2)
    side = lax.rem(me // 2, 2)
    offsets = (1 - 2 * core, 2 - 4 * side, -4, 4, 4 * side - 2, 2 * core - 1)
    lag_count, channels = lag_table.shape[0], own.shape[1]
    groups = lag_count // GROUP

    gets = [
        pltpu.make_async_copy(own_in, own, get.at[ROUNDS]),
        pltpu.make_async_copy(lag_in.at[pl.ds(tm_at[0] * lag_count, lag_count)], lag_table, get.at[ROUNDS + 1]),
    ]
    for r in range(ROUNDS):
        delta = lax.rem(partners[r] - me + count + count // 2, count) - count // 2
        role = jnp.int32(0)
        for position, offset in enumerate(offsets):
            role = role + jnp.where(delta == offset, position, 0)
        gets.append(pltpu.make_async_copy(win_in.at[role], chosen.at[r], get.at[r]))
    for copy in gets:
        copy.start()

    def turn(g, segments):
        turned = (turned_even, turned_odd)[g % 2]
        for l in range(GROUP):
            pair = lag_table[g * GROUP + l]
            cos, sin = pair[0:1], pair[1:2]
            rows = slice(l * channels, (l + 1) * channels)
            for seg in segments:
                at = 2 * seg * NB
                re, im = wide[seg, :, :NB], wide[seg, :, NB:]
                turned[rows, at:at + NB] = (re * cos - im * sin).astype(jnp.bfloat16)
                turned[rows, at + NB:at + 2 * NB] = (re * sin + im * cos).astype(jnp.bfloat16)

    gets[0].wait()
    gets[1].wait()
    total = jnp.zeros((channels, 2 * NB), jnp.float32)
    for seg in range(SEG):
        values = own[seg].astype(jnp.float32)
        wide[seg] = values
        total += values * values
    own_mean = jnp.sum(total, axis=1, keepdims=True) / (SEG * NB)
    own_scale = lax.rsqrt(own_mean + 1e-06) * (1.0 / math.sqrt(SEG * NB))
    turn(0, range(SEG))

    scales = []
    for r in range(ROUNDS):
        gets[2 + r].wait()
        squares = jnp.zeros((8, channels), jnp.float32)
        for seg in range(SEG):
            rows = chosen[r, seg].astype(jnp.float32)
            squares += jnp.sum((rows * rows).reshape(-1, 8, channels), axis=0)
        mean = jnp.sum(squares, axis=0, keepdims=True) / (SEG * NB)
        scales.append(own_scale * lax.rsqrt(mean + 1e-06))

    puts = []
    for g in range(groups):
        turned = (turned_even, turned_odd)[g % 2]
        lags = pl.ds(g * GROUP, GROUP)
        for r in range(0, ROUNDS, 2):
            right = jnp.concatenate([chosen[r + k].reshape(-1, channels) for k in range(2)], axis=1)
            sums = jnp.dot(turned[...], right, preferred_element_type=jnp.float32)
            if g + 1 < groups:
                turn(g + 1, (r, r + 1))
            for k in range(2):
                part = sums[:, k * channels:(k + 1) * channels].reshape(GROUP, channels, channels)
                staged[r + k, lags] = part * scales[r + k][None]
                copy = pltpu.make_async_copy(staged.at[r + k, lags], out.at[r + k, lags], put.at[len(puts)])
                copy.start()
                puts.append(copy)
    for copy in puts:
        copy.wait()


def local(records, band_taps, white_taps, live_mask, partners):
    segs, samples, channels = records.shape
    count = lax.axis_size("chan")
    lag_count = LAGS // lax.axis_size("tm")
    bins = bin_numbers(samples)
    period = samples // math.gcd(samples, math.gcd(int(bins[0]), int(bins[1] - bins[0])))
    cos, sin = rotation(bins[:, None] * np.arange(period)[None, :], samples)
    table = np.concatenate([cos, -sin], axis=0).astype(np.float32).astype(jnp.bfloat16)
    band_table = np.concatenate(rotation(bins[:, None] * np.arange(band_taps.shape[0])[None, :], samples), axis=1)
    white_table = np.concatenate(rotation(bins[:, None] * np.arange(white_taps.shape[0])[None, :], samples), axis=0)
    lags = 3 * (np.arange(LAGS) - LAGS // 2)
    lag_table = np.stack(rotation(lags[:, None] * bins[None, :], samples), axis=1)
    f32 = lambda a: jnp.asarray(a.astype(np.float32))
    operands = (
        records, jnp.asarray(table), f32(band_table), f32(white_table),
        band_taps.reshape(1, -1), white_taps, live_mask.reshape(1, -1),
    )

    hbm = pl.BlockSpec(memory_space=pltpu.HBM)
    smem = pl.BlockSpec(memory_space=SMEM)
    win, own_t = pl.pallas_call(
        functools.partial(gather_kernel, count, segs),
        out_shape=(
            jax.ShapeDtypeStruct((ROLES, SEG, 2 * NB, channels), jnp.bfloat16),
            jax.ShapeDtypeStruct((SEG, channels, 2 * NB), jnp.bfloat16),
        ),
        in_specs=[hbm] * len(operands),
        out_specs=(hbm, hbm),
        scratch_shapes=[
            VMEM((SEG, 2 * NB, channels), jnp.bfloat16),
            VMEM((SEG, channels, 2 * NB), jnp.bfloat16),
            VMEM(records.shape, jnp.bfloat16),
            VMEM(table.shape, jnp.bfloat16),
            VMEM(band_table.shape, jnp.float32),
            VMEM(white_table.shape, jnp.float32),
            VMEM((1, band_taps.shape[0]), jnp.float32),
            VMEM(white_taps.shape, jnp.float32),
            VMEM((1, channels), jnp.int32),
            pltpu.SemaphoreType.DMA((6 + segs,)),
            pltpu.SemaphoreType.DMA((segs + 8 * SEG,)),
            pltpu.SemaphoreType.DMA((segs,)),
            pltpu.SemaphoreType.DMA((ROLES, SEG)),
            pltpu.SemaphoreType.DMA,
        ],
        compiler_params=pltpu.CompilerParams(
            collective_id=0, has_side_effects=True, vmem_limit_bytes=WHOLE_VMEM
        ),
        name="spectra_gather",
    )(*operands)

    chan_at, tm_at = (lax.axis_index(axis).astype(jnp.int32).reshape(1) for axis in ("chan", "tm"))
    shape = (ROUNDS, lag_count, channels, channels)
    inner = SEG * 2 * NB
    return pl.pallas_call(
        functools.partial(correlate_kernel, count),
        out_shape=jax.ShapeDtypeStruct(shape, jnp.float32),
        in_specs=[smem, smem, smem, hbm, hbm, hbm],
        out_specs=hbm,
        scratch_shapes=[
            VMEM((SEG, channels, 2 * NB), jnp.bfloat16),
            VMEM((lag_count, 2, NB), jnp.float32),
            VMEM((SEG, channels, 2 * NB), jnp.float32),
            VMEM((GROUP * channels, inner), jnp.bfloat16),
            VMEM((GROUP * channels, inner), jnp.bfloat16),
            VMEM(shape, jnp.float32),
            VMEM((ROUNDS, SEG, 2 * NB, channels), jnp.bfloat16),
            pltpu.SemaphoreType.DMA((ROUNDS + 2,)),
            pltpu.SemaphoreType.DMA((ROUNDS * lag_count // GROUP,)),
        ],
        compiler_params=pltpu.CompilerParams(vmem_limit_bytes=WHOLE_VMEM),
        name="correlate",
    )(chan_at, tm_at, partners.reshape(-1), own_t, f32(lag_table), win)


def solution(mesh):
    return jax.shard_map(
        local,
        mesh=mesh,
        in_specs=(P("tm", None, "chan"), P(), P(None, "chan"), P("chan"), P(None, "chan")),
        out_specs=P(None, "tm", "chan", None),
        check_vma=False,
    )
```
